32 devices in a mesh: row: 16 (over z, y, x), col: 2 (over core).
Axes of the slice: x: 2, y: 2, z: 4, core: 2. Of those that a mesh axis runs over, the one named last changes fastest.
Arguments:
- vectors: float32 [6144, 64], P(('row', 'col')), may hold values from -6 to 6
- stiff_tiles: float32 [16, 2, 32, 192, 192], P('row', 'col'), may hold values from -0.078125 to 0.078125
- tile_coords: int32 [16, 2, 32, 2], P('row', 'col'), may hold values from 0 to 15, as said below
- tile_valid: int32 [16, 2, 32], P('row', 'col'), may hold values from 0 to 1, as said below
Outputs:
- product: float32 [6144, 64], P(('row', 'col'))
The draws below stay inside these ranges and needn't reach their ends.
Inputs may be any that keep to these rules, and one draw needn't show every extreme that they name: `tile_coords`: valid entries of a device's list are distinct and come before all padding; each list holds at most 32 valid entries, and some list holds exactly 32. A stored tile may lie on either side of the diagonal. Padding entries hold in-range coordinates. `tile_valid`: at least one entry of each list is valid.
All inputs are finite; a program needn't handle non-finite values.
Results may differ from the reference program's by a relative error of at most 0.0001.
Values sent between devices are 32-bit elements; how exact they have to be, the bound alone decides.
A program may use at most 128 MiB of HBM per device.

```python
import jax
import jax.numpy as jnp
from jax import lax

TILE = 192
VECS = 64
BLK_DEV = 1
ITERS = 2
LR = 2
LC = 16
MAXT = 32
NB = 32
N = 6144
N_ROW = 16
N_COL = 2


def tile_plan(key):
    row_count = LC // BLK_DEV
    column_count = LR // BLK_DEV
    slot_count = LR * LC
    slot_rows = jnp.arange(slot_count, dtype=jnp.int32) // LC
    slot_cols = jnp.arange(slot_count, dtype=jnp.int32) % LC

    def one_device(device):
        device_key = jax.random.fold_in(jax.random.fold_in(key, 7), device)
        perm_key, count_key = jax.random.split(device_key)
        ranking = jax.random.permutation(perm_key, slot_count).astype(jnp.int32)
        unused, order = lax.top_k(ranking, MAXT)
        power = jax.random.randint(count_key, (), 0, 4, dtype=jnp.int32)
        target = jnp.right_shift(jnp.int32(MAXT), power)
        target = jnp.where(device == 0, jnp.int32(MAXT), target)
        live_count = jnp.maximum(target, jnp.int32(1))
        live = (jnp.arange(MAXT, dtype=jnp.int32) < live_count).astype(jnp.int32)
        places = jnp.stack([slot_rows[order], slot_cols[order]], -1).astype(jnp.int32)
        return (places, live)
    places, live = jax.vmap(one_device)(jnp.arange(row_count * column_count, dtype=jnp.int32))
    return (places.reshape(row_count, column_count, MAXT, 2), live.reshape(row_count, column_count, MAXT))


def draw_tile_coords(key, part):
    return tile_plan(key)[0]


def draw_tile_valid(key, part):
    return tile_plan(key)[1]


def block_scale(key, dims, cuts, low, top_value):
    loudness = 1.0
    for position, shards_of in cuts:
        draws = jax.random.uniform(jax.random.fold_in(jax.random.fold_in(key, 6), position), (shards_of,), jnp.float32, low / len(cuts), top_value / len(cuts))
        loudness = loudness * jnp.repeat(jnp.exp(draws), dims[position] // shards_of).reshape((-1,) + (1,) * (len(dims) - 1 - position))
    return loudness


def noise(key, shape, spread, limit, shards=(), kind=jnp.bfloat16):
    result = spread * jax.random.normal(key, shape, jnp.float32)
    if shards:
        result = result * block_scale(key, shape, shards, -0.22, 0.18)
    return jnp.clip(result, -limit, limit).astype(kind)


def setup_inputs(seed: int = 0) -> dict:
    arg_keys = jax.random.split(jax.random.key(seed), 5)
    vectors = noise(arg_keys[0], (N, VECS), 1.0, 6.0, ((0, 32),), jnp.float32)
    stiff_tiles = noise(arg_keys[1], (N_ROW, N_COL, MAXT, TILE, TILE), (TILE * MAXT) ** -0.5, 0.078125, ((0, 16), (1, 2)), jnp.float32)
    tile_coords = draw_tile_coords(jax.random.fold_in(arg_keys[4], 71), 0)
    tile_valid = draw_tile_valid(jax.random.fold_in(arg_keys[4], 71), 0)
    return dict(vectors=vectors, stiff_tiles=stiff_tiles, tile_coords=tile_coords, tile_valid=tile_valid)


def reference(vectors, stiff_tiles, tile_coords, tile_valid):
    row_ids = jnp.arange(N_ROW, dtype=jnp.int32)[:, None, None]
    col_ids = jnp.arange(N_COL, dtype=jnp.int32)[None, :, None]
    local_rows = tile_coords[..., 0]
    local_cols = tile_coords[..., 1]
    global_row = row_ids * LR + local_rows
    global_col = ((local_cols // BLK_DEV) * N_COL + col_ids) * BLK_DEV + local_cols % BLK_DEV
    live_mask = tile_valid.astype(jnp.float32)
    mirror = live_mask * (global_row != global_col).astype(jnp.float32)
    devices = N_ROW * N_COL
    inputs = (stiff_tiles.reshape(devices, MAXT, TILE, TILE),
              global_row.reshape(devices, MAXT).astype(jnp.int32),
              global_col.reshape(devices, MAXT).astype(jnp.int32),
              live_mask.reshape(devices, MAXT), mirror.reshape(devices, MAXT))
    current = vectors.reshape(NB, TILE, VECS)
    for repeat in range(ITERS):
        def device_step(accumulated, pieces):
            tile_block, rows_here, cols_here, live_here, mirror_here = pieces
            right_side = current[cols_here]
            left_side = current[rows_here]
            direct = jnp.einsum("tpq,tqk->tpk", tile_block, right_side, precision=lax.Precision.HIGHEST)
            mirrored = jnp.einsum("tqp,tqk->tpk", tile_block, left_side, precision=lax.Precision.HIGHEST)
            accumulated = accumulated.at[rows_here].add(direct * live_here[:, None, None])
            accumulated = accumulated.at[cols_here].add(mirrored * mirror_here[:, None, None])
            return accumulated, None

        start_value = jnp.zeros((NB, TILE, VECS), jnp.float32)
        current, unused = lax.scan(device_step, start_value, inputs)
    return current.reshape(N, VECS)
```

```python
import functools

import jax
import jax.numpy as jnp
from jax import lax
from jax.experimental import pallas as pl
from jax.experimental.pallas import tpu as pltpu
from jax.sharding import PartitionSpec as P

ITERS = 2
MESH = pl.DeviceIdType.MESH
LANES = 128
SPLIT, KEEP, READ = range(3)
ORDER = (
    ("AP", 2, 0), ("AL", 3, 1), ("AP", 1, 0), ("AP", 1, 1), ("AP", 2, 1), ("AL", 2, 1),
    ("AL", 1, 1), ("AL", 2, 0), ("LHS",), ("C", 3), ("E", 1, 2), ("C", 2), ("E", 3, 1),
    ("AL", 1, 0), ("C", 1), ("AL", 3, 0), ("AF", 1, 2, 0), ("AT", 0, 1), ("AF", 1, 1, 0),
    ("AT", 0, 0), ("E", 3, 2), ("E", 2, 1), ("E", 1, 1), ("D", 0, 1), ("L", 3, 2), ("L", 3, 1),
    ("AF", 2, 1, 1), ("AF", 1, 1, 1), ("E", 2, 2), ("L", 2, 1), ("L", 2, 2), ("M", 3),
    ("AF", 2, 1, 0), ("AF", 1, 2, 1), ("AF", 2, 2, 1), ("AF", 2, 2, 0), ("E", 0, 2),
    ("L", 1, 2), ("AF", 3, 2, 0), ("C", 0), ("L", 1, 1), ("M", 1), ("AF", 3, 1, 0),
    ("RL", 1, 1), ("AT", 1, 1), ("E", 0, 1), ("AF", 3, 2, 1), ("RL", 3, 0), ("AF", 3, 1, 1),
    ("S", 2, 0), ("RL", 3, 1), ("M", 2), ("D", 1, 0), ("D", 3, 0), ("RL", 2, 0), ("S", 1, 0),
    ("RL", 1, 0), ("AT", 1, 0), ("RL", 2, 1), ("AT", 2, 0), ("D", 1, 2), ("AT", 2, 1),
    ("D", 1, 1), ("AT", 3, 0), ("D", 2, 1), ("AT", 3, 1), ("S", 2, 1), ("S", 1, 1), ("M", 0),
    ("D", 0, 0), ("D", 3, 2), ("D", 0, 2), ("D", 2, 0), ("D", 2, 2), ("D", 0, 3), ("D", 1, 3),
    ("D", 3, 1), ("D", 2, 3), ("G",), ("FR",), ("D", 3, 3),
)


def split(value):
    high = value.astype(jnp.bfloat16).astype(jnp.float32)
    return high, value - high


def pack_tall(value):
    half = value.shape[0] // 2
    return jnp.concatenate([value[:half], value[half:]], axis=1)


def spread(packed):
    high, low = split(packed)
    width = packed.shape[1] // 2
    left = lax.broadcasted_iota(jnp.int32, packed.shape, 1) < width
    upper = jnp.where(left, high, pltpu.roll(low, width, 1))
    lower = jnp.where(left, pltpu.roll(high, width, 1), low)
    return jnp.concatenate([upper, lower], axis=0)


def fold_tall(total):
    width = total.shape[1] // 2
    half = total.shape[0] // 2
    folded = total + pltpu.roll(total, width, 1)
    left = lax.broadcasted_iota(jnp.int32, (half, total.shape[1]), 1) < width
    return jnp.where(left, folded[:half], folded[half:])


def unpack_wide(packed, vecs, size):
    main = packed[:vecs].T
    tail = packed[vecs:]
    tail = jnp.concatenate([tail[:, : size - LANES], tail[:, size - LANES :]], axis=0).T
    return jnp.concatenate([main, tail], axis=0)


def kernel(
    rows, cols, planes, kept,
    x_hbm, coords_hbm, valid_hbm, tiles_hbm, out_ref,
    x_ref, coords, valid, table, slot_ref,
    tiles, gath, rowg, rpart, rrecv, zsend, zrecv, z2send, z2recv, lhs, total, parts,
    tile_sem, small_sem, ag_send, ag_recv, at_send, at_recv, cx_send, cx_recv, r1_send, r1_recv, rt_send, rt_recv, r2_send, r2_recv,
    cy_send, cy_recv,
):
    lines = rows // planes
    vecs, size = x_hbm.shape
    half = size // 2
    quarter = half // 2
    row = lax.axis_index("row")
    col = lax.axis_index("col")
    line = row // planes
    plane = row % planes
    up = plane // 2
    side = plane % 2

    load = pltpu.make_async_copy(tiles_hbm, tiles, tile_sem)
    small = [
        pltpu.make_async_copy(src, dst, small_sem.at[i])
        for i, (src, dst) in enumerate(((x_hbm, x_ref), (coords_hbm, coords), (valid_hbm, valid)))
    ]
    for copy in small:
        copy.start()
    load.start()

    def flipped(d):
        if d == 0:
            return plane
        if d == 1:
            return up * 2 + 1 - side
        if d == 2:
            return (1 - up) * 2 + side
        return (1 - up) * 2 + 1 - side

    def across(dz):
        spot, bit = 0, 1
        while bit < lines:
            spot = spot + (line // bit + dz // bit) % 2 * bit
            bit *= 2
        return spot

    def line_peer(dz):
        return (across(dz) * planes + plane, col)

    def plane_peer(d):
        return (line * planes + flipped(d), col)

    def col_peer(dc):
        return (row, (col + dc) % cols)

    def remote(src, dst, send, recv, where):
        return pltpu.make_async_remote_copy(
            src_ref=src, dst_ref=dst, send_sem=send, recv_sem=recv,
            device_id=where, device_id_type=MESH,
        )

    def piece(p):
        return pl.ds(p % 2 * quarter, quarter)

    def ag_line(it, dz):
        return remote(gath.at[it, 0, 0], gath.at[it, dz, 0],
                      ag_send.at[it, dz, 0, 0], ag_recv.at[it, dz, 0, 0], line_peer(dz))

    def ag_plane(it, dz, d):
        return remote(gath.at[it, dz, 0], gath.at[it, dz, d],
                      ag_send.at[it, dz, d, 0], ag_recv.at[it, dz, d, 0], plane_peer(d))

    def ag_line_half(it, dz, p):
        part = piece(p)
        return remote(gath.at[it, 0, 0, part], gath.at[it, dz, 0, part],
                      ag_send.at[it, dz, 0, p], ag_recv.at[it, dz, 0, p], line_peer(dz))

    def ag_plane_half(it, dz, d, q):
        part = piece(d - 1 + q)
        return remote(gath.at[it, dz, 0, part], gath.at[it, dz, d, part],
                      ag_send.at[it, dz, d, q], ag_recv.at[it, dz, d, q], plane_peer(d))

    def ag_pair_half(it, d, q):
        part = piece(d - 1 + q)
        return remote(gath.at[it, 0, d, part], gath.at[it, 1, d, part],
                      ag_send.at[it, 1, d, q], ag_recv.at[it, 1, d, q], line_peer(1))

    def rs_pair(it, d, q):
        part = piece(d - 1 + q)
        return remote(zsend.at[it, 1, d, part], zrecv.at[it, 1, d, part],
                      r1_send.at[it, 1, d, q], r1_recv.at[it, 1, d, q], line_peer(1))

    def rs_line_half(it, dz, p):
        part = piece(p)
        return remote(z2send.at[it, dz, part], z2recv.at[it, dz, part],
                      r2_send.at[it, dz, p], r2_recv.at[it, dz, p], line_peer(dz))

    def ag_turn(it, dz, h):
        part = pl.ds(h * quarter, quarter)
        return remote(gath.at[it, dz, 1 + h, part], gath.at[it, dz, 3, part],
                      at_send.at[it, dz, h], at_recv.at[it, dz, h], plane_peer(2 - h))

    def col_x(it, dc):
        return remote(gath.at[it, 0, 0], rowg.at[it, dc],
                      cx_send.at[it, dc], cx_recv.at[it, dc], col_peer(dc))

    def rs_turn(it, dz, h):
        part = pl.ds(h * quarter, quarter)
        return remote(zsend.at[it, dz, 3, part], zrecv.at[it, dz, 3, part],
                      rt_send.at[it, dz, h], rt_recv.at[it, dz, h], plane_peer(1 + h))

    def rs_plane(it, dz, d, late):
        part = pl.ds((d - 1 + late) % 2 * quarter, quarter)
        return remote(zsend.at[it, dz, d, part], zrecv.at[it, dz, d, part],
                      r1_send.at[it, dz, d, late], r1_recv.at[it, dz, d, late], plane_peer(d))

    def rs_line(it, dz):
        return remote(z2send.at[it, dz], z2recv.at[it, dz],
                      r2_send.at[it, dz, 0], r2_recv.at[it, dz, 0], line_peer(dz))

    def col_y(it, dc):
        return remote(rpart.at[it, dc], rrecv.at[it, dc],
                      cy_send.at[it, dc], cy_recv.at[it, dc], col_peer(dc))

    def col_s(it):
        return remote(rpart.at[it, 0], rrecv.at[it, 0],
                      cy_send.at[it, 0], cy_recv.at[it, 0], col_peer(1))

    paired = cols == 2
    planned = paired and lines == 4 and kept
    barrier = pltpu.get_barrier_semaphore()
    for dz in range(1, lines):
        pl.semaphore_signal(barrier, inc=1, device_id=line_peer(dz), device_id_type=MESH)
    for d in range(1, 3):
        pl.semaphore_signal(barrier, inc=1, device_id=plane_peer(d), device_id_type=MESH)
    for dc in range(1, cols):
        pl.semaphore_signal(barrier, inc=1, device_id=col_peer(dc), device_id_type=MESH)
    for copy in small:
        copy.wait()
    place = jnp.where(valid[...] > 0, coords[0:1, :] * rows + coords[1:2, :], -1)
    spots = (rows * cols, place.shape[1])
    hit = lax.broadcasted_iota(jnp.int32, spots, 0) == jnp.broadcast_to(place, spots)
    found = jnp.max(
        jnp.where(hit, lax.broadcasted_iota(jnp.int32, spots, 1), -1), axis=1, keepdims=True
    )
    table[...] = jnp.broadcast_to(found, table.shape)
    fill = pltpu.make_async_copy(table, slot_ref, small_sem.at[3])
    fill.start()
    gath[0, 0, 0] = pack_tall(
        jnp.concatenate([x_ref[:, :LANES].T, x_ref[:, LANES:].T], axis=0)
    )

    def split_tile(spot):
        slot = slot_ref[spot, 0]
        scale = jnp.where(slot >= 0, 1.0, 0.0).astype(jnp.float32)
        block = tiles[jnp.maximum(slot, 0)] * scale
        high = block.astype(jnp.bfloat16)
        low = (block - high.astype(jnp.float32)).astype(jnp.bfloat16)
        return high, low

    def tile_parts(a, b, mode):
        spot = a * rows + b
        if kept and mode == READ:
            return parts[spot, 0], parts[spot, 1]
        high, low = split_tile(spot)
        if kept and mode == KEEP:
            parts[spot, 0] = high
            parts[spot, 1] = low
        return high, low

    def mirrored(it, dz, d, mode=None):
        if mode is None:
            mode = KEEP if it == 0 else READ
        known = isinstance(dz, int)
        b = across(dz) * planes + flipped(d)
        acc = jnp.zeros((2 * vecs, size), jnp.float32)
        for dc in range(cols):
            if known and dz == 0 and d == 0 and dc == 0:
                continue
            a = (col - dc + cols) % cols
            high, low = tile_parts(a, b, mode)
            left = lhs[dc]
            if dc == 0 and d == 0 and not known:
                left = left * jnp.where(b == row, 0.0, 1.0).astype(jnp.bfloat16)
            acc = acc + jnp.dot(left, high, preferred_element_type=jnp.float32)
            acc = acc + jnp.dot(left, low, preferred_element_type=jnp.float32)
        wide = acc[:vecs] + acc[vecs:]
        tail = wide[:, LANES:]
        return jnp.concatenate(
            [
                wide[:, :LANES],
                jnp.concatenate([tail[: vecs // 2], tail[vecs // 2 :]], axis=1),
            ],
            axis=0,
        )

    def term(dz, d, dc, right, mode):
        b = across(dz) * planes + flipped(d)
        high, low = tile_parts((col + dc) % cols, b, mode)
        return jnp.dot(high, right, preferred_element_type=jnp.float32) + jnp.dot(
            low, right, preferred_element_type=jnp.float32
        )

    def direct(it, dz, *flips):
        sums = [None] * cols
        for d in flips:
            b = across(dz) * planes + flipped(d)
            right = spread(gath[it, dz, d]).astype(jnp.bfloat16)
            for dc in range(cols):
                high, low = tile_parts(
                    (col + dc) % cols, b, SPLIT if it == 0 and d == 0 else READ
                )
                term = jnp.dot(high, right, preferred_element_type=jnp.float32) + jnp.dot(
                    low, right, preferred_element_type=jnp.float32
                )
                sums[dc] = term if sums[dc] is None else sums[dc] + term
        for dc in range(cols):
            total[dc] += sums[dc]

    def begin(it):
        lhs[0] = spread(gath[it, 0, 0]).T.astype(jnp.bfloat16)
        total[...] = jnp.zeros_like(total)
        direct(it, 0, 0)

    seen = set()

    def access(it, dz, d):
        first = (dz, d) not in seen
        seen.add((dz, d))
        return KEEP if first else READ

    def blocked(it, dz, d, fresh=False):
        right = spread(gath[it, dz, d]).astype(jnp.bfloat16)
        mode = access(it, dz, d)
        for dc in range(cols):
            part = term(dz, d, dc, right, mode)
            if fresh:
                total[dc] = part
            else:
                total[dc] += part

    fill.wait()
    load.wait()
    if planned:
        blocked(0, 0, 0, True)
    else:
        begin(0)
    pl.semaphore_wait(barrier, (lines - 1) + 2 + (cols - 1))

    def finish_sends(it):
        def along(dz, carry):
            for p in range(2):
                ag_line_half(it, dz, p).wait_send()
                rs_line_half(it, dz, p).wait_send()
            return carry

        def within(dz, carry):
            for h in range(2):
                for d in range(1, 3):
                    ag_plane_half(it, dz, d, h).wait_send()
                    rs_plane(it, dz, d, h).wait_send()
                ag_turn(it, dz, h).wait_send()
                rs_turn(it, dz, h).wait_send()
            return carry

        lax.fori_loop(1, lines, along, 0)
        lax.fori_loop(0, lines, within, 0)

    def ordered(it):
        arrived = set()
        opening = next(task for task in ORDER if task[0] == "D")

        def once(copy, *key):
            if key not in arrived:
                arrived.add(key)
                copy(it, *key[1:]).wait_recv()

        def gathered(dz, d, q):
            if dz == 1:
                once(lambda it, dz, d, q: ag_pair_half(it, d, q), "ap", dz, d, q)
            else:
                once(ag_plane_half, "ap", dz, d, q)

        def reduced(dz, d, q):
            once(rs_plane, "rp", dz, d, q)

        def mirror(dz, d):
            return mirrored(it, dz, d, access(it, dz, d))

        if it == 0:
            for dc in range(1, cols):
                col_x(it, dc).start()
        for place, task in enumerate(ORDER):
            kind, args = task[0], task[1:]
            if it > 0 and place == len(ORDER) // 2:
                finish_sends(it - 1)
            if kind == "AL":
                ag_line_half(it, *args).start()
            elif kind == "AP":
                ag_plane_half(it, 0, *args).start()
            elif kind == "LHS":
                lhs[0] = spread(gath[it, 0, 0]).T.astype(jnp.bfloat16)
                if it == 0:
                    col_x(it, 1).wait_recv()
                    near = rowg[it, 1]
                else:
                    col_s(it - 1).wait_recv()
                    near = rrecv[it - 1, 0] + rpart[it - 1, 1]
                lhs[1] = spread(near).T.astype(jnp.bfloat16)
            elif kind == "C":
                dz, = args
                zsend[it, dz, 3] = mirror(dz, 3)
                for h in range(2):
                    rs_turn(it, dz, h).start()
            elif kind == "E":
                dz, d = args
                zsend[it, dz, d] = mirror(dz, d)
                if dz == 1:
                    rs_pair(it, d, 0).start()
                elif dz > 1:
                    rs_plane(it, dz, d, 0).start()
            elif kind == "L":
                dz, d = args
                once(rs_turn, "rt", dz, d % 2)
                zsend[it, dz, d, piece(d)] += zrecv[it, dz, 3, piece(d)]
                if dz == 1:
                    rs_pair(it, d, 1).start()
                else:
                    rs_plane(it, dz, d, 1).start()
            elif kind == "S":
                d, q = args
                part = piece(d - 1 + q)
                once(lambda it, dz, d, q: rs_pair(it, d, q), "rp", 1, d, q)
                more = zrecv[it, 1, d, part]
                if q == 1:
                    once(rs_turn, "rt", 0, d % 2)
                    more = more + zrecv[it, 0, 3, part]
                zsend[it, 0, d, part] += more
                rs_plane(it, 0, d, q).start()
            elif kind == "M":
                dz, = args
                z2send[it, dz] = mirror(dz, 0)
            elif kind == "RL":
                dz, p = args
                part = piece(p)
                if dz > 1:
                    reduced(dz, 1, p)
                    reduced(dz, 2, 1 - p)
                    z2send[it, dz, part] += zrecv[it, dz, 1, part] + zrecv[it, dz, 2, part]
                rs_line_half(it, dz, p).start()
            elif kind == "G":
                for d in range(1, 3):
                    for q in range(2):
                        reduced(0, d, q)
                z2send[it, 0] += zrecv[it, 0, 1] + zrecv[it, 0, 2]
            elif kind == "FR":
                wide = z2send[it, 0]
                for dz in range(1, lines):
                    for p in range(2):
                        once(rs_line_half, "rl", dz, p)
                    wide = wide + z2recv[it, dz]
                z2send[it, 0] = pack_tall(unpack_wide(wide, vecs, size))
            elif kind == "AF":
                dz, d, q = args
                if dz == 1:
                    gathered(0, d, q)
                    ag_pair_half(it, d, q).start()
                else:
                    once(ag_line_half, "al", dz, (d - 1 + q) % 2)
                    ag_plane_half(it, dz, d, q).start()
            elif kind == "AT":
                dz, h = args
                gathered(dz, 1 + h, 0)
                ag_turn(it, dz, h).start()
            elif it > 0 or args != (0, 0):
                dz, d = args
                if place == len(ORDER) - 1 and it == ITERS - 1:
                    finish_sends(it)
                if d == 0 and dz > 0:
                    for p in range(2):
                        once(ag_line_half, "al", dz, p)
                elif d in (1, 2):
                    for q in range(2):
                        gathered(dz, d, q)
                elif d == 3:
                    for h in range(2):
                        once(ag_turn, "at", dz, h)
                if place < len(ORDER) - 1:
                    blocked(it, dz, d, it > 0 and task == opening)
        right = spread(gath[it, dz, d]).astype(jnp.bfloat16)
        mode = access(it, dz, d)
        rpart[it, 1] = fold_tall(total[1] + term(dz, d, 1, right, mode))
        col_y(it, 1).start()
        mine = fold_tall(total[0] + term(dz, d, 0, right, mode)) + z2send[it, 0]
        if it < ITERS - 1:
            rpart[it, 0] = mine
            col_s(it).start()
        col_y(it, 1).wait_recv()
        return mine + rrecv[it, 1]

    def product(it):
        for dz in range(1, lines):
            ag_line(it, dz).start()
        fresh = it == 0 or not paired
        if fresh:
            for dc in range(1, cols):
                col_x(it, dc).start()
        for d in range(1, 3):
            ag_plane(it, 0, d).start()
        if it > 0:
            begin(it)
        if fresh:
            for dc in range(1, cols):
                col_x(it, dc).wait_recv()
                lhs[dc] = spread(rowg[it, dc]).T.astype(jnp.bfloat16)
        else:
            col_s(it - 1).wait_recv()
            near = rrecv[it - 1, 0] + rpart[it - 1, 1]
            lhs[1] = spread(near).T.astype(jnp.bfloat16)

        def corner(n, carry):
            dz = lines - 1 - n
            zsend[it, dz, 3] = mirrored(it, dz, 3)
            for h in range(2):
                rs_turn(it, dz, h).start()
            return carry

        lax.fori_loop(0, lines, corner, 0)

        def early(n, carry):
            dz = (lines - n) % lines
            for d in range(1, 3):
                zsend[it, dz, d] = mirrored(it, dz, d)
                rs_plane(it, dz, d, 0).start()
            return carry

        def late(dz):
            for d in range(1, 3):
                part = pl.ds(d % 2 * quarter, quarter)
                rs_turn(it, dz, d % 2).wait_recv()
                zsend[it, dz, d, part] += zrecv[it, dz, 3, part]
                rs_plane(it, dz, d, 1).start()

        def forward(dz, carry):
            back = lines - dz
            late(back)
            ag_line(it, dz).wait_recv()
            for d in range(1, 3):
                ag_plane(it, dz, d).start()
            z2send[it, back] = mirrored(it, back, 0)
            direct(it, dz, 0)
            return carry

        def turn(dz):
            for h in range(2):
                ag_plane(it, dz, 1 + h).wait_recv()
                ag_turn(it, dz, h).start()

        def gather_plane(dz):
            for d in range(1, 3):
                for k in range(2):
                    rs_plane(it, dz, d, k).wait_recv()
            z2send[it, dz] += zrecv[it, dz, 1] + zrecv[it, dz, 2]

        def settle(dz, carry):
            gather_plane(lines - dz)
            rs_line(it, lines - dz).start()
            turn(dz)
            direct(it, dz, 1, 2)
            return carry

        lax.fori_loop(1, lines, early, 0)
        lax.fori_loop(1, lines, forward, 0)
        early(0, 0)
        late(0)
        z2send[it, 0] = mirrored(it, 0, 0)
        turn(0)
        direct(it, 0, 1, 2)
        lax.fori_loop(1, lines, settle, 0)
        gather_plane(0)

        def last(dz, carry):
            for h in range(2):
                ag_turn(it, dz, h).wait_recv()
            direct(it, dz, 3)
            return carry

        lax.fori_loop(0, lines, last, 0)

        for dc in range(1, cols):
            rpart[it, dc] = fold_tall(total[dc])
            col_y(it, dc).start()
        mine = fold_tall(total[0])
        wide = z2send[it, 0]
        for dz in range(1, lines):
            rs_line(it, dz).wait_recv()
            wide = wide + z2recv[it, dz]
        mine = mine + pack_tall(unpack_wide(wide, vecs, size))
        if paired and it < ITERS - 1:
            rpart[it, 0] = mine
            col_s(it).start()
        for dc in range(1, cols):
            col_y(it, dc).wait_recv()
            mine = mine + rrecv[it, dc]
        return mine

    for it in range(ITERS):
        result = ordered(it) if planned else product(it)
        if it < ITERS - 1:
            gath[it + 1, 0, 0] = result
        else:
            tall = jnp.concatenate([result[:, :vecs], result[:, vecs:]], axis=0)
            out_ref[:, pl.ds(0, LANES)] = tall[:LANES].T
            out_ref[:, pl.ds(LANES, size - LANES)] = tall[LANES:].T

    for it in range(ITERS):
        for dc in range(1, cols):
            if it == 0 or not paired:
                col_x(it, dc).wait_send()
            col_y(it, dc).wait_send()
        if paired and it < ITERS - 1:
            col_s(it).wait_send()

    def drain(it, carry):
        for dz in range(1, lines):
            ag_line(it, dz).wait_send()
            rs_line(it, dz).wait_send()

        def plane_sends(dz, inner):
            for d in range(1, 3):
                ag_plane(it, dz, d).wait_send()
                for k in range(2):
                    rs_plane(it, dz, d, k).wait_send()
            for h in range(2):
                ag_turn(it, dz, h).wait_send()
                rs_turn(it, dz, h).wait_send()
            return inner

        return lax.fori_loop(0, lines, plane_sends, carry)

    if not planned:
        lax.fori_loop(0, ITERS, drain, 0)


def local(rows, cols, vectors, stiff_tiles, tile_coords, tile_valid):
    size, vecs = vectors.shape
    count = stiff_tiles.shape[2]
    planes = 4
    lines = rows // planes
    kept = rows * cols * size * size * 4 <= 16 * 1024 * 1024
    block = (size * vecs // LANES, LANES)
    f32 = jnp.float32
    dma = pltpu.SemaphoreType.DMA
    grid = (ITERS, lines, planes)
    return pl.pallas_call(
        functools.partial(kernel, rows, cols, planes, kept),
        out_shape=jax.ShapeDtypeStruct((vecs, size), f32),
        in_specs=[
            pl.BlockSpec(memory_space=pl.ANY),
            pl.BlockSpec(memory_space=pl.ANY),
            pl.BlockSpec(memory_space=pl.ANY),
            pl.BlockSpec(memory_space=pl.ANY),
        ],
        out_specs=pl.BlockSpec(memory_space=pltpu.VMEM),
        scratch_shapes=[
            pltpu.VMEM((vecs, size), f32),
            pltpu.VMEM((2, count), jnp.int32),
            pltpu.VMEM((1, count), jnp.int32),
            pltpu.VMEM((rows * cols, LANES), jnp.int32),
            pltpu.SMEM((rows * cols, LANES), jnp.int32),
            pltpu.VMEM((count, size, size), f32),
            pltpu.VMEM(grid + block, f32),
            pltpu.VMEM((ITERS, cols) + block, f32),
            pltpu.VMEM((ITERS, cols) + block, f32),
            pltpu.VMEM((ITERS, cols) + block, f32),
            pltpu.VMEM(grid + block, f32),
            pltpu.VMEM(grid + block, f32),
            pltpu.VMEM((ITERS, lines) + block, f32),
            pltpu.VMEM((ITERS, lines) + block, f32),
            pltpu.VMEM((cols, 2 * vecs, size), jnp.bfloat16),
            pltpu.VMEM((cols, size, 2 * vecs), f32),
            pltpu.VMEM((rows * cols if kept else 1, 2, size, size), jnp.bfloat16),
            dma,
            dma((4,)),
            dma(grid + (2,)), dma(grid + (2,)),
            dma((ITERS, lines, 2)), dma((ITERS, lines, 2)),
            dma((ITERS, cols)), dma((ITERS, cols)),
            dma(grid + (2,)), dma(grid + (2,)),
            dma((ITERS, lines, 2)), dma((ITERS, lines, 2)),
            dma((ITERS, lines, 2)), dma((ITERS, lines, 2)),
            dma((ITERS, cols)), dma((ITERS, cols)),
        ],
        compiler_params=pltpu.CompilerParams(
            collective_id=0, has_side_effects=True, vmem_limit_bytes=60 * 1024 * 1024
        ),
    )(vectors.T, tile_coords[0, 0].T, tile_valid[0], stiff_tiles[0, 0]).T


def solution(mesh):
    placed = (
        P(("row", "col"), None),
        P("row", "col", None, None, None),
        P("row", "col", None, None),
        P("row", "col", None),
    )
    return jax.shard_map(
        functools.partial(local, mesh.shape["row"], mesh.shape["col"]),
        mesh=mesh, in_specs=placed, out_specs=P(("row", "col"), None), check_vma=False,
    )
```

```python
import functools

import jax
import jax.numpy as jnp
from jax import lax
from jax.experimental import pallas as pl
from jax.experimental.pallas import tpu as pltpu
from jax.sharding import PartitionSpec as P

ITERS = 2
MESH = pl.DeviceIdType.MESH
LANES = 128
CHUNKS = 4
PAIR = True
ORDER = (
    ("AP", 2, 0), ("AL", 3, 1), ("AP", 1, 0), ("AP", 1, 1), ("AP", 2, 1), ("AL", 2, 1),
    ("AL", 1, 1), ("AL", 2, 0), ("LHS",), ("C", 3), ("E", 1, 2), ("C", 2), ("E", 3, 1),
    ("AL", 1, 0), ("C", 1), ("AL", 3, 0), ("AF", 1, 2, 0), ("AT", 0, 1), ("AF", 1, 1, 0),
    ("AT", 0, 0), ("E", 3, 2), ("E", 2, 1), ("E", 1, 1), ("D", 0, 1), ("L", 3, 2), ("L", 3, 1),
    ("AF", 2, 1, 1), ("AF", 1, 1, 1), ("E", 2, 2), ("L", 2, 1), ("L", 2, 2), ("M", 3),
    ("AF", 2, 1, 0), ("AF", 1, 2, 1), ("AF", 2, 2, 1), ("AF", 2, 2, 0), ("E", 0, 2),
    ("L", 1, 2), ("AF", 3, 2, 0), ("C", 0), ("L", 1, 1), ("M", 1), ("AF", 3, 1, 0),
    ("RL", 1, 1), ("AT", 1, 1), ("E", 0, 1), ("AF", 3, 2, 1), ("RL", 3, 0), ("AF", 3, 1, 1),
    ("S", 2, 0), ("RL", 3, 1), ("M", 2), ("D", 1, 0), ("D", 3, 0), ("RL", 2, 0), ("S", 1, 0),
    ("RL", 1, 0), ("AT", 1, 0), ("RL", 2, 1), ("AT", 2, 0), ("D", 1, 2), ("AT", 2, 1),
    ("D", 1, 1), ("AT", 3, 0), ("D", 2, 1), ("AT", 3, 1), ("S", 2, 1), ("S", 1, 1), ("M", 0),
    ("D", 0, 0), ("D", 3, 2), ("D", 0, 2), ("D", 2, 0), ("D", 2, 2), ("D", 0, 3), ("D", 1, 3),
    ("D", 3, 1), ("D", 2, 3), ("G",), ("FR",), ("D", 3, 3),
)


def split(value):
    high = value.astype(jnp.bfloat16).astype(jnp.float32)
    return high, value - high


def pack_tall(value):
    half = value.shape[0] // 2
    return jnp.concatenate([value[:half], value[half:]], axis=1)


def spread(packed):
    high, low = split(packed)
    width = packed.shape[1] // 2
    left = lax.broadcasted_iota(jnp.int32, packed.shape, 1) < width
    upper = jnp.where(left, high, pltpu.roll(low, width, 1))
    lower = jnp.where(left, pltpu.roll(high, width, 1), low)
    return jnp.concatenate([upper, lower], axis=0)


def fold_tall(total):
    width = total.shape[1] // 2
    half = total.shape[0] // 2
    folded = total + pltpu.roll(total, width, 1)
    left = lax.broadcasted_iota(jnp.int32, (half, total.shape[1]), 1) < width
    return jnp.where(left, folded[:half], folded[half:])


def unpack_wide(packed, vecs, size):
    main = packed[:vecs].T
    tail = packed[vecs:]
    tail = jnp.concatenate([tail[:, : size - LANES], tail[:, size - LANES :]], axis=0).T
    return jnp.concatenate([main, tail], axis=0)


def kernel(
    rows, cols, planes, kept,
    x_hbm, coords_hbm, valid_hbm, tiles_hbm, out_ref,
    x_ref, coords, valid, table, slot_ref,
    tiles, gath, rowg, rpart, rrecv, zsend, zrecv, z2send, z2recv, lhs, total, parts, stack, tile_sem,
    small_sem, ag_send, ag_recv, at_send, at_recv, cx_send, cx_recv, r1_send, r1_recv, rt_send, rt_recv, r2_send, r2_recv,
    cy_send, cy_recv,
):
    lines = rows // planes
    vecs, size = x_hbm.shape
    half = size // 2
    quarter = half // 2
    row = lax.axis_index("row")
    col = lax.axis_index("col")
    line = row // planes
    plane = row % planes
    up = plane // 2
    side = plane % 2

    count = tiles.shape[0]
    share = count // CHUNKS
    spans = [
        pl.ds(i * share, share if i < CHUNKS - 1 else count - i * share) for i in range(CHUNKS)
    ]
    loads = [
        pltpu.make_async_copy(tiles_hbm.at[span], tiles.at[span], tile_sem.at[i])
        for i, span in enumerate(spans)
    ]
    small = [
        pltpu.make_async_copy(src, dst, small_sem.at[i])
        for i, (src, dst) in enumerate(((x_hbm, x_ref), (coords_hbm, coords), (valid_hbm, valid)))
    ]

    def flipped(d):
        if d == 0:
            return plane
        if d == 1:
            return up * 2 + 1 - side
        if d == 2:
            return (1 - up) * 2 + side
        return (1 - up) * 2 + 1 - side

    def across(dz):
        spot, bit = 0, 1
        while bit < lines:
            spot = spot + (line // bit + dz // bit) % 2 * bit
            bit *= 2
        return spot

    def line_peer(dz):
        return (across(dz) * planes + plane, col)

    def plane_peer(d):
        return (line * planes + flipped(d), col)

    def col_peer(dc):
        return (row, (col + dc) % cols)

    def remote(src, dst, send, recv, where):
        return pltpu.make_async_remote_copy(
            src_ref=src, dst_ref=dst, send_sem=send, recv_sem=recv,
            device_id=where, device_id_type=MESH,
        )

    def piece(p):
        return pl.ds(p % 2 * quarter, quarter)

    def ag_line(it, dz):
        return remote(gath.at[it, 0, 0], gath.at[it, dz, 0],
                      ag_send.at[it, dz, 0, 0], ag_recv.at[it, dz, 0, 0], line_peer(dz))

    def ag_plane(it, dz, d):
        return remote(gath.at[it, dz, 0], gath.at[it, dz, d],
                      ag_send.at[it, dz, d, 0], ag_recv.at[it, dz, d, 0], plane_peer(d))

    def ag_line_half(it, dz, p):
        part = piece(p)
        return remote(gath.at[it, 0, 0, part], gath.at[it, dz, 0, part],
                      ag_send.at[it, dz, 0, p], ag_recv.at[it, dz, 0, p], line_peer(dz))

    def ag_plane_half(it, dz, d, q):
        part = piece(d - 1 + q)
        return remote(gath.at[it, dz, 0, part], gath.at[it, dz, d, part],
                      ag_send.at[it, dz, d, q], ag_recv.at[it, dz, d, q], plane_peer(d))

    def ag_pair_half(it, d, q):
        part = piece(d - 1 + q)
        return remote(gath.at[it, 0, d, part], gath.at[it, 1, d, part],
                      ag_send.at[it, 1, d, q], ag_recv.at[it, 1, d, q], line_peer(1))

    def rs_pair(it, d, q):
        part = piece(d - 1 + q)
        return remote(zsend.at[it, 1, d, part], zrecv.at[it, 1, d, part],
                      r1_send.at[it, 1, d, q], r1_recv.at[it, 1, d, q], line_peer(1))

    def rs_line_half(it, dz, p):
        part = piece(p)
        return remote(z2send.at[it, dz, part], z2recv.at[it, dz, part],
                      r2_send.at[it, dz, p], r2_recv.at[it, dz, p], line_peer(dz))

    def ag_turn(it, dz, h):
        part = pl.ds(h * quarter, quarter)
        return remote(gath.at[it, dz, 1 + h, part], gath.at[it, dz, 3, part],
                      at_send.at[it, dz, h], at_recv.at[it, dz, h], plane_peer(2 - h))

    def col_x(it, dc):
        return remote(gath.at[it, 0, 0], rowg.at[it, dc],
                      cx_send.at[it, dc], cx_recv.at[it, dc], col_peer(dc))

    def rs_turn(it, dz, h):
        part = pl.ds(h * quarter, quarter)
        return remote(zsend.at[it, dz, 3, part], zrecv.at[it, dz, 3, part],
                      rt_send.at[it, dz, h], rt_recv.at[it, dz, h], plane_peer(1 + h))

    def rs_plane(it, dz, d, late):
        part = pl.ds((d - 1 + late) % 2 * quarter, quarter)
        return remote(zsend.at[it, dz, d, part], zrecv.at[it, dz, d, part],
                      r1_send.at[it, dz, d, late], r1_recv.at[it, dz, d, late], plane_peer(d))

    def rs_line(it, dz):
        return remote(z2send.at[it, dz], z2recv.at[it, dz],
                      r2_send.at[it, dz, 0], r2_recv.at[it, dz, 0], line_peer(dz))

    def col_y(it, dc):
        return remote(rpart.at[it, dc], rrecv.at[it, dc],
                      cy_send.at[it, dc], cy_recv.at[it, dc], col_peer(dc))

    def col_s(it):
        return remote(rpart.at[it, 0], rrecv.at[it, 0],
                      cy_send.at[it, 0], cy_recv.at[it, 0], col_peer(1))

    paired = cols == 2
    planned = kept
    barrier = pltpu.get_barrier_semaphore()
    for dz in range(1, lines):
        pl.semaphore_signal(barrier, inc=1, device_id=line_peer(dz), device_id_type=MESH)
    for d in range(1, 3):
        pl.semaphore_signal(barrier, inc=1, device_id=plane_peer(d), device_id_type=MESH)
    for dc in range(1, cols):
        pl.semaphore_signal(barrier, inc=1, device_id=col_peer(dc), device_id_type=MESH)
    for copy in small:
        copy.start()
    for load in loads:
        load.start()
    for copy in small:
        copy.wait()
    place = jnp.where(valid[...] > 0, coords[0:1, :] * rows + coords[1:2, :], -1)
    spots = (rows * cols, place.shape[1])
    hit = lax.broadcasted_iota(jnp.int32, spots, 0) == jnp.broadcast_to(place, spots)
    found = jnp.max(
        jnp.where(hit, lax.broadcasted_iota(jnp.int32, spots, 1), -1), axis=1, keepdims=True
    )
    table[...] = jnp.broadcast_to(found, table.shape)
    fill = pltpu.make_async_copy(table, slot_ref, small_sem.at[3])
    fill.start()
    gath[0, 0, 0] = pack_tall(
        jnp.concatenate([x_ref[:, :LANES].T, x_ref[:, LANES:].T], axis=0)
    )

    def split_tile(spot):
        slot = slot_ref[spot, 0]
        scale = jnp.where(slot >= 0, 1.0, 0.0).astype(jnp.float32)
        block = tiles[jnp.maximum(slot, 0)] * scale
        high = block.astype(jnp.bfloat16)
        low = (block - high.astype(jnp.float32)).astype(jnp.bfloat16)
        return high, low

    def stored(a, b):
        slot = slot_ref[a * rows + b, 0]
        return jnp.where(slot >= 0, slot, count)

    def folded(acc):
        wide = acc[:vecs] + acc[vecs:]
        tail = wide[:, LANES:]
        return jnp.concatenate(
            [
                wide[:, :LANES],
                jnp.concatenate([tail[: vecs // 2], tail[vecs // 2 :]], axis=1),
            ],
            axis=0,
        )

    def mirrored(it, dz, d):
        b = across(dz) * planes + flipped(d)
        if planned:
            spots = [stored(a, b) for a in range(cols)]
            if dz == 0 and d == 0:
                spots = [jnp.where(col == a, count, spots[a]) for a in range(cols)]
            right = jnp.concatenate([parts[spot] for spot in spots], axis=0)
            return folded(jnp.dot(stack[...], right, preferred_element_type=jnp.float32))
        acc = jnp.zeros((2 * vecs, size), jnp.float32)
        for dc in range(cols):
            high, low = split_tile((col - dc + cols) % cols * rows + b)
            left = lhs[dc]
            if dc == 0 and d == 0:
                left = left * jnp.where(b == row, 0.0, 1.0).astype(jnp.bfloat16)
            acc = acc + jnp.dot(left, high, preferred_element_type=jnp.float32)
            acc = acc + jnp.dot(left, low, preferred_element_type=jnp.float32)
        return folded(acc)

    def terms(dz, d, right, *shifts):
        b = across(dz) * planes + flipped(d)
        result = []
        for dc in shifts:
            both = jnp.dot(
                parts[stored((col + dc) % cols, b)], right, preferred_element_type=jnp.float32
            )
            result.append(both[:size] + both[size:])
        return result

    def direct(it, dz, *flips):
        sums = [None] * cols
        for d in flips:
            b = across(dz) * planes + flipped(d)
            right = spread(gath[it, dz, d]).astype(jnp.bfloat16)
            for dc in range(cols):
                high, low = split_tile((col + dc) % cols * rows + b)
                term = jnp.dot(high, right, preferred_element_type=jnp.float32) + jnp.dot(
                    low, right, preferred_element_type=jnp.float32
                )
                sums[dc] = term if sums[dc] is None else sums[dc] + term
        for dc in range(cols):
            total[dc] += sums[dc]

    def begin(it):
        lhs[0] = spread(gath[it, 0, 0]).T.astype(jnp.bfloat16)
        total[...] = jnp.zeros_like(total)
        direct(it, 0, 0)

    def blocked(it, dz, d, fresh=False):
        right = spread(gath[it, dz, d]).astype(jnp.bfloat16)
        for dc, part in enumerate(terms(dz, d, right, *range(cols))):
            if fresh:
                total[dc] = part
            else:
                total[dc] += part

    if planned:
        parts[count] = jnp.zeros((2 * size, size), jnp.bfloat16)
        for i, load in enumerate(loads):
            load.wait()

            def cut(slot, carry):
                block = tiles[slot]
                high = block.astype(jnp.bfloat16)
                parts[slot, pl.ds(0, size)] = high
                parts[slot, pl.ds(size, size)] = (block - high.astype(jnp.float32)).astype(
                    jnp.bfloat16
                )
                return carry

            lax.fori_loop(i * share, (i + 1) * share, cut, 0)
        fill.wait()
        blocked(0, 0, 0, True)
    else:
        for load in loads:
            load.wait()
        fill.wait()
        begin(0)
    pl.semaphore_wait(barrier, (lines - 1) + 2 + (cols - 1))

    def finish_sends(it):
        def along(dz, carry):
            for p in range(2):
                ag_line_half(it, dz, p).wait_send()
                rs_line_half(it, dz, p).wait_send()
            return carry

        def within(dz, carry):
            for h in range(2):
                for d in range(1, 3):
                    ag_plane_half(it, dz, d, h).wait_send()
                    rs_plane(it, dz, d, h).wait_send()
                ag_turn(it, dz, h).wait_send()
                rs_turn(it, dz, h).wait_send()
            return carry

        lax.fori_loop(1, lines, along, 0)
        lax.fori_loop(0, lines, within, 0)

    def ordered(it):
        arrived = set()
        opening = next(task for task in ORDER if task[0] == "D")

        def once(copy, *key):
            if key not in arrived:
                arrived.add(key)
                copy(it, *key[1:]).wait_recv()

        def gathered(dz, d, q):
            if PAIR and dz == 1:
                once(lambda it, dz, d, q: ag_pair_half(it, d, q), "ap", dz, d, q)
            else:
                once(ag_plane_half, "ap", dz, d, q)

        def reduced(dz, d, q):
            once(rs_plane, "rp", dz, d, q)

        if it == 0:
            for dc in range(1, cols):
                col_x(it, dc).start()
        for place, task in enumerate(ORDER):
            kind, args = task[0], task[1:]
            if it > 0 and place == len(ORDER) // 2:
                finish_sends(it - 1)
            if kind == "AL":
                ag_line_half(it, *args).start()
            elif kind == "AP":
                ag_plane_half(it, 0, *args).start()
            elif kind == "LHS":
                own = spread(gath[it, 0, 0]).T.astype(jnp.bfloat16)
                if it == 0:
                    col_x(it, 1).wait_recv()
                    near = rowg[it, 1]
                else:
                    col_s(it - 1).wait_recv()
                    near = rrecv[it - 1, 0] + rpart[it - 1, 1]
                near = spread(near).T.astype(jnp.bfloat16)
                first = jnp.where(col == 0, own, near)
                second = jnp.where(col == 0, near, own)
                stack[...] = jnp.concatenate([first, first, second, second], axis=1)
            elif kind == "C":
                dz, = args
                zsend[it, dz, 3] = mirrored(it, dz, 3)
                for h in range(2):
                    rs_turn(it, dz, h).start()
            elif kind == "E":
                dz, d = args
                zsend[it, dz, d] = mirrored(it, dz, d)
                if PAIR and dz == 1:
                    rs_pair(it, d, 0).start()
                elif dz > 0 or not PAIR:
                    rs_plane(it, dz, d, 0).start()
            elif kind == "L":
                dz, d = args
                once(rs_turn, "rt", dz, d % 2)
                zsend[it, dz, d, piece(d)] += zrecv[it, dz, 3, piece(d)]
                if PAIR and dz == 1:
                    rs_pair(it, d, 1).start()
                else:
                    rs_plane(it, dz, d, 1).start()
            elif kind == "S":
                d, q = args
                part = piece(d - 1 + q)
                once(lambda it, dz, d, q: rs_pair(it, d, q), "rp", 1, d, q)
                more = zrecv[it, 1, d, part]
                if q == 1:
                    once(rs_turn, "rt", 0, d % 2)
                    more = more + zrecv[it, 0, 3, part]
                zsend[it, 0, d, part] += more
                rs_plane(it, 0, d, q).start()
            elif kind == "M":
                dz, = args
                z2send[it, dz] = mirrored(it, dz, 0)
            elif kind == "RL":
                dz, p = args
                part = piece(p)
                if dz > 1 or not PAIR:
                    reduced(dz, 1, p)
                    reduced(dz, 2, 1 - p)
                    z2send[it, dz, part] += zrecv[it, dz, 1, part] + zrecv[it, dz, 2, part]
                rs_line_half(it, dz, p).start()
            elif kind == "G":
                for d in range(1, 3):
                    for q in range(2):
                        reduced(0, d, q)
                z2send[it, 0] += zrecv[it, 0, 1] + zrecv[it, 0, 2]
            elif kind == "FR":
                wide = z2send[it, 0]
                for dz in range(1, lines):
                    for p in range(2):
                        once(rs_line_half, "rl", dz, p)
                    wide = wide + z2recv[it, dz]
                z2send[it, 0] = pack_tall(unpack_wide(wide, vecs, size))
            elif kind == "AF":
                dz, d, q = args
                if PAIR and dz == 1:
                    gathered(0, d, q)
                    ag_pair_half(it, d, q).start()
                else:
                    once(ag_line_half, "al", dz, (d - 1 + q) % 2)
                    ag_plane_half(it, dz, d, q).start()
            elif kind == "AT":
                dz, h = args
                gathered(dz, 1 + h, 0)
                ag_turn(it, dz, h).start()
            elif it > 0 or args != (0, 0):
                dz, d = args
                if place == len(ORDER) - 1 and it == ITERS - 1:
                    finish_sends(it)
                if d == 0 and dz > 0:
                    for p in range(2):
                        once(ag_line_half, "al", dz, p)
                elif d in (1, 2):
                    for q in range(2):
                        gathered(dz, d, q)
                elif d == 3:
                    for h in range(2):
                        once(ag_turn, "at", dz, h)
                if place < len(ORDER) - 1:
                    blocked(it, dz, d, it > 0 and task == opening)
        right = spread(gath[it, dz, d]).astype(jnp.bfloat16)
        rpart[it, 1] = fold_tall(total[1] + terms(dz, d, right, 1)[0])
        col_y(it, 1).start()
        mine = fold_tall(total[0] + terms(dz, d, right, 0)[0]) + z2send[it, 0]
        if it < ITERS - 1:
            rpart[it, 0] = mine
            col_s(it).start()
        col_y(it, 1).wait_recv()
        return mine + rrecv[it, 1]

    def product(it):
        for dz in range(1, lines):
            ag_line(it, dz).start()
        fresh = it == 0 or not paired
        if fresh:
            for dc in range(1, cols):
                col_x(it, dc).start()
        for d in range(1, 3):
            ag_plane(it, 0, d).start()
        if it > 0:
            begin(it)
        if fresh:
            for dc in range(1, cols):
                col_x(it, dc).wait_recv()
                lhs[dc] = spread(rowg[it, dc]).T.astype(jnp.bfloat16)
        else:
            col_s(it - 1).wait_recv()
            near = rrecv[it - 1, 0] + rpart[it - 1, 1]
            lhs[1] = spread(near).T.astype(jnp.bfloat16)

        def corner(n, carry):
            dz = lines - 1 - n
            zsend[it, dz, 3] = mirrored(it, dz, 3)
            for h in range(2):
                rs_turn(it, dz, h).start()
            return carry

        lax.fori_loop(0, lines, corner, 0)

        def early(n, carry):
            dz = (lines - n) % lines
            for d in range(1, 3):
                zsend[it, dz, d] = mirrored(it, dz, d)
                rs_plane(it, dz, d, 0).start()
            return carry

        def late(dz):
            for d in range(1, 3):
                part = pl.ds(d % 2 * quarter, quarter)
                rs_turn(it, dz, d % 2).wait_recv()
                zsend[it, dz, d, part] += zrecv[it, dz, 3, part]
                rs_plane(it, dz, d, 1).start()

        def forward(dz, carry):
            back = lines - dz
            late(back)
            ag_line(it, dz).wait_recv()
            for d in range(1, 3):
                ag_plane(it, dz, d).start()
            z2send[it, back] = mirrored(it, back, 0)
            direct(it, dz, 0)
            return carry

        def turn(dz):
            for h in range(2):
                ag_plane(it, dz, 1 + h).wait_recv()
                ag_turn(it, dz, h).start()

        def gather_plane(dz):
            for d in range(1, 3):
                for k in range(2):
                    rs_plane(it, dz, d, k).wait_recv()
            z2send[it, dz] += zrecv[it, dz, 1] + zrecv[it, dz, 2]

        def settle(dz, carry):
            gather_plane(lines - dz)
            rs_line(it, lines - dz).start()
            turn(dz)
            direct(it, dz, 1, 2)
            return carry

        lax.fori_loop(1, lines, early, 0)
        lax.fori_loop(1, lines, forward, 0)
        early(0, 0)
        late(0)
        z2send[it, 0] = mirrored(it, 0, 0)
        turn(0)
        direct(it, 0, 1, 2)
        lax.fori_loop(1, lines, settle, 0)
        gather_plane(0)

        def last(dz, carry):
            for h in range(2):
                ag_turn(it, dz, h).wait_recv()
            direct(it, dz, 3)
            return carry

        lax.fori_loop(0, lines, last, 0)

        for dc in range(1, cols):
            rpart[it, dc] = fold_tall(total[dc])
            col_y(it, dc).start()
        mine = fold_tall(total[0])
        wide = z2send[it, 0]
        for dz in range(1, lines):
            rs_line(it, dz).wait_recv()
            wide = wide + z2recv[it, dz]
        mine = mine + pack_tall(unpack_wide(wide, vecs, size))
        if paired and it < ITERS - 1:
            rpart[it, 0] = mine
            col_s(it).start()
        for dc in range(1, cols):
            col_y(it, dc).wait_recv()
            mine = mine + rrecv[it, dc]
        return mine

    for it in range(ITERS):
        result = ordered(it) if planned else product(it)
        if it < ITERS - 1:
            gath[it + 1, 0, 0] = result
        else:
            tall = jnp.concatenate([result[:, :vecs], result[:, vecs:]], axis=0)
            out_ref[:, pl.ds(0, LANES)] = tall[:LANES].T
            out_ref[:, pl.ds(LANES, size - LANES)] = tall[LANES:].T

    for it in range(ITERS):
        for dc in range(1, cols):
            if it == 0 or not paired:
                col_x(it, dc).wait_send()
            col_y(it, dc).wait_send()
        if paired and it < ITERS - 1:
            col_s(it).wait_send()

    def drain(it, carry):
        for dz in range(1, lines):
            ag_line(it, dz).wait_send()
            rs_line(it, dz).wait_send()

        def plane_sends(dz, inner):
            for d in range(1, 3):
                ag_plane(it, dz, d).wait_send()
                for k in range(2):
                    rs_plane(it, dz, d, k).wait_send()
            for h in range(2):
                ag_turn(it, dz, h).wait_send()
                rs_turn(it, dz, h).wait_send()
            return inner

        return lax.fori_loop(0, lines, plane_sends, carry)

    if not planned:
        lax.fori_loop(0, ITERS, drain, 0)


def local(rows, cols, vectors, stiff_tiles, tile_coords, tile_valid):
    size, vecs = vectors.shape
    count = stiff_tiles.shape[2]
    planes = 4
    lines = rows // planes
    kept = lines == 4 and cols == 2 and count % CHUNKS == 0 and count <= 64
    block = (size * vecs // LANES, LANES)
    f32 = jnp.float32
    dma = pltpu.SemaphoreType.DMA
    grid = (ITERS, lines, planes)
    return pl.pallas_call(
        functools.partial(kernel, rows, cols, planes, kept),
        out_shape=pltpu.VMEM((vecs, size), f32),
        in_specs=[
            pl.BlockSpec(memory_space=pl.ANY),
            pl.BlockSpec(memory_space=pl.ANY),
            pl.BlockSpec(memory_space=pl.ANY),
            pl.BlockSpec(memory_space=pl.ANY),
        ],
        out_specs=pl.BlockSpec(memory_space=pltpu.VMEM),
        scratch_shapes=[
            pltpu.VMEM((vecs, size), f32),
            pltpu.VMEM((2, count), jnp.int32),
            pltpu.VMEM((1, count), jnp.int32),
            pltpu.VMEM((rows * cols, LANES), jnp.int32),
            pltpu.SMEM((rows * cols, LANES), jnp.int32),
            pltpu.VMEM((count, size, size), f32),
            pltpu.VMEM(grid + block, f32),
            pltpu.VMEM((ITERS, cols) + block, f32),
            pltpu.VMEM((ITERS, cols) + block, f32),
            pltpu.VMEM((ITERS, cols) + block, f32),
            pltpu.VMEM(grid + block, f32),
            pltpu.VMEM(grid + block, f32),
            pltpu.VMEM((ITERS, lines) + block, f32),
            pltpu.VMEM((ITERS, lines) + block, f32),
            pltpu.VMEM((cols, 2 * vecs, size), jnp.bfloat16),
            pltpu.VMEM((cols, size, 2 * vecs), f32),
            pltpu.VMEM((count + 1 if kept else 1, 2 * size, size), jnp.bfloat16),
            pltpu.VMEM((2 * vecs, 4 * size), jnp.bfloat16),
            dma((CHUNKS,)),
            dma((4,)),
            dma(grid + (2,)), dma(grid + (2,)),
            dma((ITERS, lines, 2)), dma((ITERS, lines, 2)),
            dma((ITERS, cols)), dma((ITERS, cols)),
            dma(grid + (2,)), dma(grid + (2,)),
            dma((ITERS, lines, 2)), dma((ITERS, lines, 2)),
            dma((ITERS, lines, 2)), dma((ITERS, lines, 2)),
            dma((ITERS, cols)), dma((ITERS, cols)),
        ],
        compiler_params=pltpu.CompilerParams(
            collective_id=0, has_side_effects=True, vmem_limit_bytes=60 * 1024 * 1024
        ),
    )(vectors.T, tile_coords[0, 0].T, tile_valid[0], stiff_tiles[0, 0]).T


def solution(mesh):
    placed = (
        P(("row", "col"), None),
        P("row", "col", None, None, None),
        P("row", "col", None, None),
        P("row", "col", None),
    )
    return jax.shard_map(
        functools.partial(local, mesh.shape["row"], mesh.shape["col"]),
        mesh=mesh, in_specs=placed, out_specs=P(("row", "col"), None), check_vma=False,
    )
```

```python
import functools

import jax
import jax.numpy as jnp
from jax import lax
from jax.experimental import pallas as pl
from jax.experimental.pallas import tpu as pltpu
from jax.sharding import PartitionSpec as P

ITERS = 2
MESH = pl.DeviceIdType.MESH
LANES = 128
CHUNKS = 4
PAIR = True
RS_DIAG = ()
AG_DIAG = ()
ORDER = (
    ("AP", 2, 0), ("AL", 2, 1), ("AL", 2, 0), ("AL", 1, 0), ("AP", 1, 0), ("AP", 2, 1),
    ("AP", 1, 1), ("AL", 3, 0), ("LHS",), ("C", 3), ("C", 2), ("AL", 1, 1), ("E", 3, 2),
    ("AL", 3, 1), ("E", 3, 1), ("C", 0), ("D", 0, 0), ("C", 1), ("E", 1, 1), ("E", 1, 2),
    ("E", 0, 1), ("L", 3, 1), ("AF", 2, 2, 0), ("AF", 1, 2, 0), ("L", 3, 2), ("AF", 1, 1, 0),
    ("AF", 1, 1, 1), ("AT", 0, 1), ("AF", 2, 1, 0), ("E", 2, 2), ("E", 2, 1), ("M", 1),
    ("L", 2, 2), ("M", 2), ("AF", 1, 2, 1), ("AF", 2, 2, 1), ("L", 2, 1), ("L", 1, 1), ("M", 0),
    ("AF", 3, 1, 1), ("L", 1, 2), ("AF", 3, 2, 0), ("M", 3), ("AF", 3, 1, 0), ("RL", 3, 1),
    ("RL", 1, 1), ("AT", 2, 1), ("D", 3, 0), ("AF", 3, 2, 1), ("RL", 3, 0), ("AT", 0, 0),
    ("D", 0, 1), ("AF", 2, 1, 1), ("E", 0, 2), ("AT", 2, 0), ("RL", 2, 0), ("AT", 1, 1),
    ("S", 1, 0), ("AT", 1, 0), ("S", 2, 0), ("D", 1, 2), ("RL", 1, 0), ("RL", 2, 1),
    ("D", 2, 2), ("S", 1, 1), ("S", 2, 1), ("AT", 3, 0), ("D", 2, 0), ("AT", 3, 1), ("D", 3, 2),
    ("D", 0, 2), ("D", 2, 1), ("D", 1, 1), ("D", 0, 3), ("D", 2, 3), ("D", 1, 0), ("D", 3, 1),
    ("D", 1, 3), ("G",), ("FR",), ("D", 3, 3),
)


def split(value):
    high = value.astype(jnp.bfloat16).astype(jnp.float32)
    return high, value - high


def pack_tall(value):
    half = value.shape[0] // 2
    return jnp.concatenate([value[:half], value[half:]], axis=1)


def spread(packed):
    high, low = split(packed)
    width = packed.shape[1] // 2
    left = lax.broadcasted_iota(jnp.int32, packed.shape, 1) < width
    upper = jnp.where(left, high, pltpu.roll(low, width, 1))
    lower = jnp.where(left, pltpu.roll(high, width, 1), low)
    return jnp.concatenate([upper, lower], axis=0)


def fold_tall(total):
    width = total.shape[1] // 2
    half = total.shape[0] // 2
    folded = total + pltpu.roll(total, width, 1)
    left = lax.broadcasted_iota(jnp.int32, (half, total.shape[1]), 1) < width
    return jnp.where(left, folded[:half], folded[half:])


def unpack_wide(packed, vecs, size):
    main = packed[:vecs].T
    tail = packed[vecs:]
    tail = jnp.concatenate([tail[:, : size - LANES], tail[:, size - LANES :]], axis=0).T
    return jnp.concatenate([main, tail], axis=0)


def kernel(
    rows, cols, planes, kept,
    x_hbm, coords_hbm, valid_hbm, tiles_hbm, out_ref,
    x_ref, coords, valid, table, slot_ref,
    tiles, gath, rowg, rpart, rrecv, zsend, zrecv, z2send, z2recv, lhs, total, parts, stack, tile_sem,
    small_sem, ag_send, ag_recv, at_send, at_recv, cx_send, cx_recv, r1_send, r1_recv, rt_send, rt_recv, r2_send, r2_recv,
    cy_send, cy_recv,
):
    lines = rows // planes
    vecs, size = x_hbm.shape
    half = size // 2
    quarter = half // 2
    row = lax.axis_index("row")
    col = lax.axis_index("col")
    line = row // planes
    plane = row % planes
    up = plane // 2
    side = plane % 2

    count = tiles.shape[0]
    share = count // CHUNKS
    spans = [
        pl.ds(i * share, share if i < CHUNKS - 1 else count - i * share) for i in range(CHUNKS)
    ]
    loads = [
        pltpu.make_async_copy(tiles_hbm.at[span], tiles.at[span], tile_sem.at[i])
        for i, span in enumerate(spans)
    ]
    small = [
        pltpu.make_async_copy(src, dst, small_sem.at[i])
        for i, (src, dst) in enumerate(((x_hbm, x_ref), (coords_hbm, coords), (valid_hbm, valid)))
    ]

    def flipped(d):
        if d == 0:
            return plane
        if d == 1:
            return up * 2 + 1 - side
        if d == 2:
            return (1 - up) * 2 + side
        return (1 - up) * 2 + 1 - side

    def across(dz):
        spot, bit = 0, 1
        while bit < lines:
            spot = spot + (line // bit + dz // bit) % 2 * bit
            bit *= 2
        return spot

    def line_peer(dz):
        return (across(dz) * planes + plane, col)

    def plane_peer(d):
        return (line * planes + flipped(d), col)

    def col_peer(dc):
        return (row, (col + dc) % cols)

    def remote(src, dst, send, recv, where):
        return pltpu.make_async_remote_copy(
            src_ref=src, dst_ref=dst, send_sem=send, recv_sem=recv,
            device_id=where, device_id_type=MESH,
        )

    def piece(p):
        return pl.ds(p % 2 * quarter, quarter)

    def ag_line(it, dz):
        return remote(gath.at[it, 0, 0], gath.at[it, dz, 0],
                      ag_send.at[it, dz, 0, 0], ag_recv.at[it, dz, 0, 0], line_peer(dz))

    def ag_plane(it, dz, d):
        return remote(gath.at[it, dz, 0], gath.at[it, dz, d],
                      ag_send.at[it, dz, d, 0], ag_recv.at[it, dz, d, 0], plane_peer(d))

    def ag_line_half(it, dz, p):
        part = piece(p)
        return remote(gath.at[it, 0, 0, part], gath.at[it, dz, 0, part],
                      ag_send.at[it, dz, 0, p], ag_recv.at[it, dz, 0, p], line_peer(dz))

    def ag_plane_half(it, dz, d, q):
        part = piece(d - 1 + q)
        return remote(gath.at[it, dz, 0, part], gath.at[it, dz, d, part],
                      ag_send.at[it, dz, d, q], ag_recv.at[it, dz, d, q], plane_peer(d))

    def ag_pair_half(it, d, q):
        part = piece(d - 1 + q)
        return remote(gath.at[it, 0, d, part], gath.at[it, 1, d, part],
                      ag_send.at[it, 1, d, q], ag_recv.at[it, 1, d, q], line_peer(1))

    def rs_pair(it, d, q):
        part = piece(d - 1 + q)
        return remote(zsend.at[it, 1, d, part], zrecv.at[it, 1, d, part],
                      r1_send.at[it, 1, d, q], r1_recv.at[it, 1, d, q], line_peer(1))

    def rs_diag(it, dz):
        return remote(zsend.at[it, dz, 3], zrecv.at[it, dz, 3],
                      r1_send.at[it, dz, 3, 0], r1_recv.at[it, dz, 3, 0], plane_peer(3))

    def ag_diag(it, dz):
        return remote(gath.at[it, dz, 0], gath.at[it, dz, 3],
                      ag_send.at[it, dz, 3, 0], ag_recv.at[it, dz, 3, 0], plane_peer(3))

    def rs_line_half(it, dz, p):
        part = piece(p)
        return remote(z2send.at[it, dz, part], z2recv.at[it, dz, part],
                      r2_send.at[it, dz, p], r2_recv.at[it, dz, p], line_peer(dz))

    def ag_turn(it, dz, h):
        part = pl.ds(h * quarter, quarter)
        return remote(gath.at[it, dz, 1 + h, part], gath.at[it, dz, 3, part],
                      at_send.at[it, dz, h], at_recv.at[it, dz, h], plane_peer(2 - h))

    def col_x(it, dc):
        return remote(gath.at[it, 0, 0], rowg.at[it, dc],
                      cx_send.at[it, dc], cx_recv.at[it, dc], col_peer(dc))

    def rs_turn(it, dz, h):
        part = pl.ds(h * quarter, quarter)
        return remote(zsend.at[it, dz, 3, part], zrecv.at[it, dz, 3, part],
                      rt_send.at[it, dz, h], rt_recv.at[it, dz, h], plane_peer(1 + h))

    def rs_plane(it, dz, d, late):
        part = pl.ds((d - 1 + late) % 2 * quarter, quarter)
        return remote(zsend.at[it, dz, d, part], zrecv.at[it, dz, d, part],
                      r1_send.at[it, dz, d, late], r1_recv.at[it, dz, d, late], plane_peer(d))

    def rs_line(it, dz):
        return remote(z2send.at[it, dz], z2recv.at[it, dz],
                      r2_send.at[it, dz, 0], r2_recv.at[it, dz, 0], line_peer(dz))

    def col_y(it, dc):
        return remote(rpart.at[it, dc], rrecv.at[it, dc],
                      cy_send.at[it, dc], cy_recv.at[it, dc], col_peer(dc))

    def col_s(it):
        return remote(rpart.at[it, 0], rrecv.at[it, 0],
                      cy_send.at[it, 0], cy_recv.at[it, 0], col_peer(1))

    paired = cols == 2
    planned = kept
    barrier = pltpu.get_barrier_semaphore()
    for dz in range(1, lines):
        pl.semaphore_signal(barrier, inc=1, device_id=line_peer(dz), device_id_type=MESH)
    for d in range(1, 3):
        pl.semaphore_signal(barrier, inc=1, device_id=plane_peer(d), device_id_type=MESH)
    for dc in range(1, cols):
        pl.semaphore_signal(barrier, inc=1, device_id=col_peer(dc), device_id_type=MESH)
    for copy in small:
        copy.start()
    for load in loads:
        load.start()
    for copy in small:
        copy.wait()
    place = jnp.where(valid[...] > 0, coords[0:1, :] * rows + coords[1:2, :], -1)
    spots = (rows * cols, place.shape[1])
    hit = lax.broadcasted_iota(jnp.int32, spots, 0) == jnp.broadcast_to(place, spots)
    found = jnp.max(
        jnp.where(hit, lax.broadcasted_iota(jnp.int32, spots, 1), -1), axis=1, keepdims=True
    )
    table[...] = jnp.broadcast_to(found, table.shape)
    fill = pltpu.make_async_copy(table, slot_ref, small_sem.at[3])
    fill.start()
    gath[0, 0, 0] = pack_tall(
        jnp.concatenate([x_ref[:, :LANES].T, x_ref[:, LANES:].T], axis=0)
    )

    def split_tile(spot):
        slot = slot_ref[spot, 0]
        scale = jnp.where(slot >= 0, 1.0, 0.0).astype(jnp.float32)
        block = tiles[jnp.maximum(slot, 0)] * scale
        high = block.astype(jnp.bfloat16)
        low = (block - high.astype(jnp.float32)).astype(jnp.bfloat16)
        return high, low

    def stored(a, b):
        slot = slot_ref[a * rows + b, 0]
        return jnp.where(slot >= 0, slot, count)

    def folded(acc):
        wide = acc[:vecs] + acc[vecs:]
        tail = wide[:, LANES:]
        return jnp.concatenate(
            [
                wide[:, :LANES],
                jnp.concatenate([tail[: vecs // 2], tail[vecs // 2 :]], axis=1),
            ],
            axis=0,
        )

    def mirrored(it, dz, d):
        b = across(dz) * planes + flipped(d)
        if planned:
            spots = [stored(a, b) for a in range(cols)]
            if dz == 0 and d == 0:
                spots = [jnp.where(col == a, count, spots[a]) for a in range(cols)]
            right = jnp.concatenate([parts[spot] for spot in spots], axis=0)
            return folded(jnp.dot(stack[...], right, preferred_element_type=jnp.float32))
        acc = jnp.zeros((2 * vecs, size), jnp.float32)
        for dc in range(cols):
            high, low = split_tile((col - dc + cols) % cols * rows + b)
            left = lhs[dc]
            if dc == 0 and d == 0:
                left = left * jnp.where(b == row, 0.0, 1.0).astype(jnp.bfloat16)
            acc = acc + jnp.dot(left, high, preferred_element_type=jnp.float32)
            acc = acc + jnp.dot(left, low, preferred_element_type=jnp.float32)
        return folded(acc)

    def terms(dz, d, right, *shifts):
        b = across(dz) * planes + flipped(d)
        result = []
        for dc in shifts:
            both = jnp.dot(
                parts[stored((col + dc) % cols, b)], right, preferred_element_type=jnp.float32
            )
            result.append(both[:size] + both[size:])
        return result

    def direct(it, dz, *flips):
        sums = [None] * cols
        for d in flips:
            b = across(dz) * planes + flipped(d)
            right = spread(gath[it, dz, d]).astype(jnp.bfloat16)
            for dc in range(cols):
                high, low = split_tile((col + dc) % cols * rows + b)
                term = jnp.dot(high, right, preferred_element_type=jnp.float32) + jnp.dot(
                    low, right, preferred_element_type=jnp.float32
                )
                sums[dc] = term if sums[dc] is None else sums[dc] + term
        for dc in range(cols):
            total[dc] += sums[dc]

    def begin(it):
        lhs[0] = spread(gath[it, 0, 0]).T.astype(jnp.bfloat16)
        total[...] = jnp.zeros_like(total)
        direct(it, 0, 0)

    def blocked(it, dz, d, fresh=False):
        right = spread(gath[it, dz, d]).astype(jnp.bfloat16)
        for dc, part in enumerate(terms(dz, d, right, *range(cols))):
            if fresh:
                total[dc] = part
            else:
                total[dc] += part

    if planned:
        parts[count] = jnp.zeros((2 * size, size), jnp.bfloat16)
        for i, load in enumerate(loads):
            load.wait()

            def cut(slot, carry):
                block = tiles[slot]
                high = block.astype(jnp.bfloat16)
                parts[slot, pl.ds(0, size)] = high
                parts[slot, pl.ds(size, size)] = (block - high.astype(jnp.float32)).astype(
                    jnp.bfloat16
                )
                return carry

            lax.fori_loop(i * share, (i + 1) * share, cut, 0)
        fill.wait()
        blocked(0, 0, 0, True)
    else:
        for load in loads:
            load.wait()
        fill.wait()
        begin(0)
    pl.semaphore_wait(barrier, (lines - 1) + 2 + (cols - 1))

    def finish_sends(it):
        for dz in range(lines):
            for h in range(2):
                if dz > 0:
                    ag_line_half(it, dz, h).wait_send()
                    rs_line_half(it, dz, h).wait_send()
                for d in range(1, 3):
                    ag_plane_half(it, dz, d, h).wait_send()
                    rs_plane(it, dz, d, h).wait_send()
                if dz not in AG_DIAG:
                    ag_turn(it, dz, h).wait_send()
                if dz not in RS_DIAG:
                    rs_turn(it, dz, h).wait_send()
            if dz in AG_DIAG:
                ag_diag(it, dz).wait_send()
            if dz in RS_DIAG:
                rs_diag(it, dz).wait_send()

    def ordered(it):
        arrived = set()
        opening = next(task for task in ORDER if task[0] == "D")

        def once(copy, *key):
            if key not in arrived:
                arrived.add(key)
                copy(it, *key[1:]).wait_recv()

        def gathered(dz, d, q):
            if PAIR and dz == 1:
                once(lambda it, dz, d, q: ag_pair_half(it, d, q), "ap", dz, d, q)
            else:
                once(ag_plane_half, "ap", dz, d, q)

        def reduced(dz, d, q):
            once(rs_plane, "rp", dz, d, q)

        if it == 0:
            for dc in range(1, cols):
                col_x(it, dc).start()
        for place, task in enumerate(ORDER):
            kind, args = task[0], task[1:]
            if it > 0 and place == len(ORDER) // 2:
                finish_sends(it - 1)
            if kind == "AL":
                ag_line_half(it, *args).start()
            elif kind == "AP":
                ag_plane_half(it, 0, *args).start()
            elif kind == "LHS":
                own = spread(gath[it, 0, 0]).T.astype(jnp.bfloat16)
                if it == 0:
                    col_x(it, 1).wait_recv()
                    near = rowg[it, 1]
                else:
                    col_s(it - 1).wait_recv()
                    near = rrecv[it - 1, 0] + rpart[it - 1, 1]
                near = spread(near).T.astype(jnp.bfloat16)
                first = jnp.where(col == 0, own, near)
                second = jnp.where(col == 0, near, own)
                stack[...] = jnp.concatenate([first, first, second, second], axis=1)
            elif kind == "C":
                dz, = args
                zsend[it, dz, 3] = mirrored(it, dz, 3)
                if dz in RS_DIAG:
                    rs_diag(it, dz).start()
                else:
                    for h in range(2):
                        rs_turn(it, dz, h).start()
            elif kind == "E":
                dz, d = args
                zsend[it, dz, d] = mirrored(it, dz, d)
                for q in range(2 if dz in RS_DIAG else 1):
                    if PAIR and dz == 1:
                        rs_pair(it, d, q).start()
                    elif dz > 0 or not PAIR:
                        rs_plane(it, dz, d, q).start()
            elif kind == "L":
                dz, d = args
                once(rs_turn, "rt", dz, d % 2)
                zsend[it, dz, d, piece(d)] += zrecv[it, dz, 3, piece(d)]
                if PAIR and dz == 1:
                    rs_pair(it, d, 1).start()
                else:
                    rs_plane(it, dz, d, 1).start()
            elif kind == "S":
                d, q = args
                part = piece(d - 1 + q)
                once(lambda it, dz, d, q: rs_pair(it, d, q), "rp", 1, d, q)
                more = zrecv[it, 1, d, part]
                if q == 1 and 0 not in RS_DIAG:
                    once(rs_turn, "rt", 0, d % 2)
                    more = more + zrecv[it, 0, 3, part]
                zsend[it, 0, d, part] += more
                rs_plane(it, 0, d, q).start()
            elif kind == "M":
                dz, = args
                z2send[it, dz] = mirrored(it, dz, 0)
            elif kind == "RL":
                dz, p = args
                part = piece(p)
                if dz > 1 or not PAIR:
                    reduced(dz, 1, p)
                    reduced(dz, 2, 1 - p)
                    z2send[it, dz, part] += zrecv[it, dz, 1, part] + zrecv[it, dz, 2, part]
                if dz in RS_DIAG:
                    once(rs_diag, "rd", dz)
                    z2send[it, dz, part] += zrecv[it, dz, 3, part]
                rs_line_half(it, dz, p).start()
            elif kind == "G":
                for d in range(1, 3):
                    for q in range(2):
                        reduced(0, d, q)
                z2send[it, 0] += zrecv[it, 0, 1] + zrecv[it, 0, 2]
                if 0 in RS_DIAG:
                    once(rs_diag, "rd", 0)
                    z2send[it, 0] += zrecv[it, 0, 3]
            elif kind == "FR":
                wide = z2send[it, 0]
                for dz in range(1, lines):
                    for p in range(2):
                        once(rs_line_half, "rl", dz, p)
                    wide = wide + z2recv[it, dz]
                z2send[it, 0] = pack_tall(unpack_wide(wide, vecs, size))
            elif kind == "AF":
                dz, d, q = args
                if PAIR and dz == 1:
                    gathered(0, d, q)
                    ag_pair_half(it, d, q).start()
                else:
                    once(ag_line_half, "al", dz, (d - 1 + q) % 2)
                    ag_plane_half(it, dz, d, q).start()
            elif kind == "AT":
                dz, h = args
                gathered(dz, 1 + h, 0)
                ag_turn(it, dz, h).start()
            elif kind == "AD":
                dz, = args
                if dz > 0:
                    for p in range(2):
                        once(ag_line_half, "al", dz, p)
                ag_diag(it, dz).start()
            elif it > 0 or args != (0, 0):
                dz, d = args
                if place == len(ORDER) - 1 and it == ITERS - 1:
                    finish_sends(it)
                if d == 0 and dz > 0:
                    for p in range(2):
                        once(ag_line_half, "al", dz, p)
                elif d in (1, 2):
                    for q in range(2):
                        gathered(dz, d, q)
                elif d == 3 and dz in AG_DIAG:
                    once(ag_diag, "ad", dz)
                elif d == 3:
                    for h in range(2):
                        once(ag_turn, "at", dz, h)
                if place < len(ORDER) - 1:
                    blocked(it, dz, d, it > 0 and task == opening)
        right = spread(gath[it, dz, d]).astype(jnp.bfloat16)
        rpart[it, 1] = fold_tall(total[1] + terms(dz, d, right, 1)[0])
        col_y(it, 1).start()
        mine = fold_tall(total[0] + terms(dz, d, right, 0)[0]) + z2send[it, 0]
        if it < ITERS - 1:
            rpart[it, 0] = mine
            col_s(it).start()
        col_y(it, 1).wait_recv()
        return mine + rrecv[it, 1]

    def product(it):
        for dz in range(1, lines):
            ag_line(it, dz).start()
        fresh = it == 0 or not paired
        if fresh:
            for dc in range(1, cols):
                col_x(it, dc).start()
        for d in range(1, 3):
            ag_plane(it, 0, d).start()
        if it > 0:
            begin(it)
        if fresh:
            for dc in range(1, cols):
                col_x(it, dc).wait_recv()
                lhs[dc] = spread(rowg[it, dc]).T.astype(jnp.bfloat16)
        else:
            col_s(it - 1).wait_recv()
            near = rrecv[it - 1, 0] + rpart[it - 1, 1]
            lhs[1] = spread(near).T.astype(jnp.bfloat16)

        def corner(n, carry):
            dz = lines - 1 - n
            zsend[it, dz, 3] = mirrored(it, dz, 3)
            for h in range(2):
                rs_turn(it, dz, h).start()
            return carry

        lax.fori_loop(0, lines, corner, 0)

        def early(n, carry):
            dz = (lines - n) % lines
            for d in range(1, 3):
                zsend[it, dz, d] = mirrored(it, dz, d)
                rs_plane(it, dz, d, 0).start()
            return carry

        def late(dz):
            for d in range(1, 3):
                part = pl.ds(d % 2 * quarter, quarter)
                rs_turn(it, dz, d % 2).wait_recv()
                zsend[it, dz, d, part] += zrecv[it, dz, 3, part]
                rs_plane(it, dz, d, 1).start()

        def forward(dz, carry):
            back = lines - dz
            late(back)
            ag_line(it, dz).wait_recv()
            for d in range(1, 3):
                ag_plane(it, dz, d).start()
            z2send[it, back] = mirrored(it, back, 0)
            direct(it, dz, 0)
            return carry

        def turn(dz):
            for h in range(2):
                ag_plane(it, dz, 1 + h).wait_recv()
                ag_turn(it, dz, h).start()

        def gather_plane(dz):
            for d in range(1, 3):
                for k in range(2):
                    rs_plane(it, dz, d, k).wait_recv()
            z2send[it, dz] += zrecv[it, dz, 1] + zrecv[it, dz, 2]

        def settle(dz, carry):
            gather_plane(lines - dz)
            rs_line(it, lines - dz).start()
            turn(dz)
            direct(it, dz, 1, 2)
            return carry

        lax.fori_loop(1, lines, early, 0)
        lax.fori_loop(1, lines, forward, 0)
        early(0, 0)
        late(0)
        z2send[it, 0] = mirrored(it, 0, 0)
        turn(0)
        direct(it, 0, 1, 2)
        lax.fori_loop(1, lines, settle, 0)
        gather_plane(0)

        def last(dz, carry):
            for h in range(2):
                ag_turn(it, dz, h).wait_recv()
            direct(it, dz, 3)
            return carry

        lax.fori_loop(0, lines, last, 0)

        for dc in range(1, cols):
            rpart[it, dc] = fold_tall(total[dc])
            col_y(it, dc).start()
        mine = fold_tall(total[0])
        wide = z2send[it, 0]
        for dz in range(1, lines):
            rs_line(it, dz).wait_recv()
            wide = wide + z2recv[it, dz]
        mine = mine + pack_tall(unpack_wide(wide, vecs, size))
        if paired and it < ITERS - 1:
            rpart[it, 0] = mine
            col_s(it).start()
        for dc in range(1, cols):
            col_y(it, dc).wait_recv()
            mine = mine + rrecv[it, dc]
        return mine

    for it in range(ITERS):
        result = ordered(it) if planned else product(it)
        if it < ITERS - 1:
            gath[it + 1, 0, 0] = result
        else:
            tall = jnp.concatenate([result[:, :vecs], result[:, vecs:]], axis=0)
            out_ref[:, pl.ds(0, LANES)] = tall[:LANES].T
            out_ref[:, pl.ds(LANES, size - LANES)] = tall[LANES:].T

    for it in range(ITERS):
        for dc in range(1, cols):
            if it == 0 or not paired:
                col_x(it, dc).wait_send()
            col_y(it, dc).wait_send()
        if paired and it < ITERS - 1:
            col_s(it).wait_send()

    def drain(it, carry):
        for dz in range(1, lines):
            ag_line(it, dz).wait_send()
            rs_line(it, dz).wait_send()

        def plane_sends(dz, inner):
            for d in range(1, 3):
                ag_plane(it, dz, d).wait_send()
                for k in range(2):
                    rs_plane(it, dz, d, k).wait_send()
            for h in range(2):
                ag_turn(it, dz, h).wait_send()
                rs_turn(it, dz, h).wait_send()
            return inner

        return lax.fori_loop(0, lines, plane_sends, carry)

    if not planned:
        lax.fori_loop(0, ITERS, drain, 0)


def local(rows, cols, vectors, stiff_tiles, tile_coords, tile_valid):
    size, vecs = vectors.shape
    count = stiff_tiles.shape[2]
    planes = 4
    lines = rows // planes
    kept = lines == 4 and cols == 2 and count % CHUNKS == 0 and count <= 64
    block = (size * vecs // LANES, LANES)
    f32 = jnp.float32
    dma = pltpu.SemaphoreType.DMA
    grid = (ITERS, lines, planes)
    return pl.pallas_call(
        functools.partial(kernel, rows, cols, planes, kept),
        out_shape=pltpu.VMEM((vecs, size), f32),
        in_specs=[
            pl.BlockSpec(memory_space=pl.ANY),
            pl.BlockSpec(memory_space=pl.ANY),
            pl.BlockSpec(memory_space=pl.ANY),
            pl.BlockSpec(memory_space=pl.ANY),
        ],
        out_specs=pl.BlockSpec(memory_space=pltpu.VMEM),
        scratch_shapes=[
            pltpu.VMEM((vecs, size), f32),
            pltpu.VMEM((2, count), jnp.int32),
            pltpu.VMEM((1, count), jnp.int32),
            pltpu.VMEM((rows * cols, LANES), jnp.int32),
            pltpu.SMEM((rows * cols, LANES), jnp.int32),
            pltpu.VMEM((count, size, size), f32),
            pltpu.VMEM(grid + block, f32),
            pltpu.VMEM((ITERS, cols) + block, f32),
            pltpu.VMEM((ITERS, cols) + block, f32),
            pltpu.VMEM((ITERS, cols) + block, f32),
            pltpu.VMEM(grid + block, f32),
            pltpu.VMEM(grid + block, f32),
            pltpu.VMEM((ITERS, lines) + block, f32),
            pltpu.VMEM((ITERS, lines) + block, f32),
            pltpu.VMEM((cols, 2 * vecs, size), jnp.bfloat16),
            pltpu.VMEM((cols, size, 2 * vecs), f32),
            pltpu.VMEM((count + 1 if kept else 1, 2 * size, size), jnp.bfloat16),
            pltpu.VMEM((2 * vecs, 4 * size), jnp.bfloat16),
            dma((CHUNKS,)),
            dma((4,)),
            dma(grid + (2,)), dma(grid + (2,)),
            dma((ITERS, lines, 2)), dma((ITERS, lines, 2)),
            dma((ITERS, cols)), dma((ITERS, cols)),
            dma(grid + (2,)), dma(grid + (2,)),
            dma((ITERS, lines, 2)), dma((ITERS, lines, 2)),
            dma((ITERS, lines, 2)), dma((ITERS, lines, 2)),
            dma((ITERS, cols)), dma((ITERS, cols)),
        ],
        compiler_params=pltpu.CompilerParams(
            collective_id=0, has_side_effects=True, vmem_limit_bytes=60 * 1024 * 1024
        ),
    )(vectors.T, tile_coords[0, 0].T, tile_valid[0], stiff_tiles[0, 0]).T


def solution(mesh):
    placed = (
        P(("row", "col"), None),
        P("row", "col", None, None, None),
        P("row", "col", None, None),
        P("row", "col", None),
    )
    return jax.shard_map(
        functools.partial(local, mesh.shape["row"], mesh.shape["col"]),
        mesh=mesh, in_specs=placed, out_specs=P(("row", "col"), None), check_vma=False,
    )
```

```python
import functools

import jax
import jax.numpy as jnp
from jax import lax
from jax.experimental import pallas as pl
from jax.experimental.pallas import tpu as pltpu
from jax.sharding import PartitionSpec as P

ITERS = 2
MESH = pl.DeviceIdType.MESH
LANES = 128
CHUNKS = 4
PAIR = True
RS_DIAG = ()
AG_DIAG = ()
ORDER = (
    ("AP", 2, 0), ("AL", 2, 1), ("AL", 2, 0), ("AL", 1, 0), ("AP", 1, 0), ("AP", 2, 1),
    ("AP", 1, 1), ("AL", 3, 0), ("LHS",), ("C", 3), ("C", 2), ("AL", 1, 1), ("E", 3, 2),
    ("AL", 3, 1), ("E", 3, 1), ("C", 0), ("D", 0, 0), ("C", 1), ("E", 1, 1), ("E", 1, 2),
    ("E", 0, 1), ("L", 3, 1), ("AF", 2, 2, 0), ("AF", 1, 2, 0), ("L", 3, 2), ("AF", 1, 1, 0),
    ("AF", 1, 1, 1), ("AT", 0, 1), ("AF", 2, 1, 0), ("E", 2, 2), ("E", 2, 1), ("M", 1),
    ("L", 2, 2), ("M", 2), ("AF", 1, 2, 1), ("AF", 2, 2, 1), ("L", 2, 1), ("L", 1, 1), ("M", 0),
    ("AF", 3, 1, 1), ("L", 1, 2), ("AF", 3, 2, 0), ("M", 3), ("AF", 3, 1, 0), ("RL", 3, 1),
    ("RL", 1, 1), ("AT", 2, 1), ("D", 3, 0), ("AF", 3, 2, 1), ("RL", 3, 0), ("AT", 0, 0),
    ("D", 0, 1), ("AF", 2, 1, 1), ("E", 0, 2), ("AT", 2, 0), ("RL", 2, 0), ("AT", 1, 1),
    ("S", 1, 0), ("AT", 1, 0), ("S", 2, 0), ("D", 1, 2), ("RL", 1, 0), ("RL", 2, 1),
    ("D", 2, 2), ("S", 1, 1), ("S", 2, 1), ("AT", 3, 0), ("D", 2, 0), ("AT", 3, 1), ("D", 3, 2),
    ("D", 0, 2), ("D", 2, 1), ("D", 1, 1), ("D", 0, 3), ("D", 2, 3), ("D", 1, 0), ("D", 3, 1),
    ("D", 1, 3), ("G",), ("FR",), ("D", 3, 3),
)


def split(value):
    high = value.astype(jnp.bfloat16).astype(jnp.float32)
    return high, value - high


def pack_tall(value):
    half = value.shape[0] // 2
    return jnp.concatenate([value[:half], value[half:]], axis=1)


def spread(packed):
    high, low = split(packed)
    width = packed.shape[1] // 2
    left = lax.broadcasted_iota(jnp.int32, packed.shape, 1) < width
    upper = jnp.where(left, high, pltpu.roll(low, width, 1))
    lower = jnp.where(left, pltpu.roll(high, width, 1), low)
    return jnp.concatenate([upper, lower], axis=0)


def fold_tall(total):
    width = total.shape[1] // 2
    half = total.shape[0] // 2
    folded = total + pltpu.roll(total, width, 1)
    left = lax.broadcasted_iota(jnp.int32, (half, total.shape[1]), 1) < width
    return jnp.where(left, folded[:half], folded[half:])


def unpack_wide(packed, vecs, size):
    main = packed[:vecs].T
    tail = packed[vecs:]
    tail = jnp.concatenate([tail[:, : size - LANES], tail[:, size - LANES :]], axis=0).T
    return jnp.concatenate([main, tail], axis=0)


def kernel(
    rows, cols, planes, kept,
    x_hbm, coords_hbm, valid_hbm, tiles_hbm, out_ref,
    x_ref, coords, valid, table, slot_ref,
    tiles, gath, rowg, rpart, rrecv, zsend, zrecv, z2send, z2recv, lhs, total, parts, stack, tile_sem,
    small_sem, ag_send, ag_recv, at_send, at_recv, cx_send, cx_recv, r1_send, r1_recv, rt_send, rt_recv, r2_send, r2_recv,
    cy_send, cy_recv,
):
    lines = rows // planes
    vecs, size = x_hbm.shape
    half = size // 2
    quarter = half // 2
    row = lax.axis_index("row")
    col = lax.axis_index("col")
    line = row // planes
    plane = row % planes
    up = plane // 2
    side = plane % 2

    count = tiles.shape[0]
    share = count // CHUNKS
    spans = [
        pl.ds(i * share, share if i < CHUNKS - 1 else count - i * share) for i in range(CHUNKS)
    ]
    loads = [
        pltpu.make_async_copy(tiles_hbm.at[span], tiles.at[span], tile_sem.at[i])
        for i, span in enumerate(spans)
    ]
    small = [
        pltpu.make_async_copy(src, dst, small_sem.at[i])
        for i, (src, dst) in enumerate(((x_hbm, x_ref), (coords_hbm, coords), (valid_hbm, valid)))
    ]

    def flipped(d):
        if d == 0:
            return plane
        if d == 1:
            return up * 2 + 1 - side
        if d == 2:
            return (1 - up) * 2 + side
        return (1 - up) * 2 + 1 - side

    def across(dz):
        spot, bit = 0, 1
        while bit < lines:
            spot = spot + (line // bit + dz // bit) % 2 * bit
            bit *= 2
        return spot

    def line_peer(dz):
        return (across(dz) * planes + plane, col)

    def plane_peer(d):
        return (line * planes + flipped(d), col)

    def col_peer(dc):
        return (row, (col + dc) % cols)

    def remote(src, dst, send, recv, where):
        return pltpu.make_async_remote_copy(
            src_ref=src, dst_ref=dst, send_sem=send, recv_sem=recv,
            device_id=where, device_id_type=MESH,
        )

    def piece(p):
        return pl.ds(p % 2 * quarter, quarter)

    def ag_line(it, dz):
        return remote(gath.at[it, 0, 0], gath.at[it, dz, 0],
                      ag_send.at[it, dz, 0, 0], ag_recv.at[it, dz, 0, 0], line_peer(dz))

    def ag_plane(it, dz, d):
        return remote(gath.at[it, dz, 0], gath.at[it, dz, d],
                      ag_send.at[it, dz, d, 0], ag_recv.at[it, dz, d, 0], plane_peer(d))

    def ag_line_half(it, dz, p):
        part = piece(p)
        return remote(gath.at[it, 0, 0, part], gath.at[it, dz, 0, part],
                      ag_send.at[it, dz, 0, p], ag_recv.at[it, dz, 0, p], line_peer(dz))

    def ag_plane_half(it, dz, d, q):
        part = piece(d - 1 + q)
        return remote(gath.at[it, dz, 0, part], gath.at[it, dz, d, part],
                      ag_send.at[it, dz, d, q], ag_recv.at[it, dz, d, q], plane_peer(d))

    def ag_pair_half(it, d, q):
        part = piece(d - 1 + q)
        return remote(gath.at[it, 0, d, part], gath.at[it, 1, d, part],
                      ag_send.at[it, 1, d, q], ag_recv.at[it, 1, d, q], line_peer(1))

    def rs_pair(it, d, q):
        part = piece(d - 1 + q)
        return remote(zsend.at[it, 1, d, part], zrecv.at[it, 1, d, part],
                      r1_send.at[it, 1, d, q], r1_recv.at[it, 1, d, q], line_peer(1))

    def rs_diag(it, dz):
        return remote(zsend.at[it, dz, 3], zrecv.at[it, dz, 3],
                      r1_send.at[it, dz, 3, 0], r1_recv.at[it, dz, 3, 0], plane_peer(3))

    def ag_diag(it, dz):
        return remote(gath.at[it, dz, 0], gath.at[it, dz, 3],
                      ag_send.at[it, dz, 3, 0], ag_recv.at[it, dz, 3, 0], plane_peer(3))

    def rs_line_half(it, dz, p):
        part = piece(p)
        return remote(z2send.at[it, dz, part], z2recv.at[it, dz, part],
                      r2_send.at[it, dz, p], r2_recv.at[it, dz, p], line_peer(dz))

    def ag_turn(it, dz, h):
        part = pl.ds(h * quarter, quarter)
        return remote(gath.at[it, dz, 1 + h, part], gath.at[it, dz, 3, part],
                      at_send.at[it, dz, h], at_recv.at[it, dz, h], plane_peer(2 - h))

    def col_x(it, dc):
        return remote(gath.at[it, 0, 0], rowg.at[it, dc],
                      cx_send.at[it, dc], cx_recv.at[it, dc], col_peer(dc))

    def rs_turn(it, dz, h):
        part = pl.ds(h * quarter, quarter)
        return remote(zsend.at[it, dz, 3, part], zrecv.at[it, dz, 3, part],
                      rt_send.at[it, dz, h], rt_recv.at[it, dz, h], plane_peer(1 + h))

    def rs_plane(it, dz, d, late):
        part = pl.ds((d - 1 + late) % 2 * quarter, quarter)
        return remote(zsend.at[it, dz, d, part], zrecv.at[it, dz, d, part],
                      r1_send.at[it, dz, d, late], r1_recv.at[it, dz, d, late], plane_peer(d))

    def rs_line(it, dz):
        return remote(z2send.at[it, dz], z2recv.at[it, dz],
                      r2_send.at[it, dz, 0], r2_recv.at[it, dz, 0], line_peer(dz))

    def col_y(it, dc):
        return remote(rpart.at[it, dc], rrecv.at[it, dc],
                      cy_send.at[it, dc], cy_recv.at[it, dc], col_peer(dc))

    def col_s(it):
        return remote(rpart.at[it, 0], rrecv.at[it, 0],
                      cy_send.at[it, 0], cy_recv.at[it, 0], col_peer(1))

    paired = cols == 2
    planned = kept
    barrier = pltpu.get_barrier_semaphore()
    for dz in range(1, lines):
        pl.semaphore_signal(barrier, inc=1, device_id=line_peer(dz), device_id_type=MESH)
    for d in range(1, 3):
        pl.semaphore_signal(barrier, inc=1, device_id=plane_peer(d), device_id_type=MESH)
    for dc in range(1, cols):
        pl.semaphore_signal(barrier, inc=1, device_id=col_peer(dc), device_id_type=MESH)
    for copy in small:
        copy.start()
    for load in loads:
        load.start()
    for copy in small:
        copy.wait()
    place = jnp.where(valid[...] > 0, coords[0:1, :] * rows + coords[1:2, :], -1)
    spots = (rows * cols, place.shape[1])
    hit = lax.broadcasted_iota(jnp.int32, spots, 0) == jnp.broadcast_to(place, spots)
    found = jnp.max(
        jnp.where(hit, lax.broadcasted_iota(jnp.int32, spots, 1), -1), axis=1, keepdims=True
    )
    table[...] = jnp.broadcast_to(found, table.shape)
    fill = pltpu.make_async_copy(table, slot_ref, small_sem.at[3])
    fill.start()
    gath[0, 0, 0] = pack_tall(
        jnp.concatenate([x_ref[:, :LANES].T, x_ref[:, LANES:].T], axis=0)
    )

    def split_tile(spot):
        slot = slot_ref[spot, 0]
        scale = jnp.where(slot >= 0, 1.0, 0.0).astype(jnp.float32)
        block = tiles[jnp.maximum(slot, 0)] * scale
        high = block.astype(jnp.bfloat16)
        low = (block - high.astype(jnp.float32)).astype(jnp.bfloat16)
        return high, low

    def stored(a, b):
        slot = slot_ref[a * rows + b, 0]
        return jnp.where(slot >= 0, slot, count)

    def folded(acc):
        wide = acc[:vecs] + acc[vecs:]
        tail = wide[:, LANES:]
        return jnp.concatenate(
            [
                wide[:, :LANES],
                jnp.concatenate([tail[: vecs // 2], tail[vecs // 2 :]], axis=1),
            ],
            axis=0,
        )

    def mirrored(it, dz, d):
        b = across(dz) * planes + flipped(d)
        if planned:
            spots = [stored(a, b) for a in range(cols)]
            if dz == 0 and d == 0:
                spots = [jnp.where(col == a, count, spots[a]) for a in range(cols)]
            right = jnp.concatenate([parts[spot] for spot in spots], axis=0)
            return folded(jnp.dot(stack[...], right, preferred_element_type=jnp.float32))
        acc = jnp.zeros((2 * vecs, size), jnp.float32)
        for dc in range(cols):
            high, low = split_tile((col - dc + cols) % cols * rows + b)
            left = lhs[dc]
            if dc == 0 and d == 0:
                left = left * jnp.where(b == row, 0.0, 1.0).astype(jnp.bfloat16)
            acc = acc + jnp.dot(left, high, preferred_element_type=jnp.float32)
            acc = acc + jnp.dot(left, low, preferred_element_type=jnp.float32)
        return folded(acc)

    def terms(dz, d, right, *shifts):
        b = across(dz) * planes + flipped(d)
        result = []
        for dc in shifts:
            both = jnp.dot(
                parts[stored((col + dc) % cols, b)], right, preferred_element_type=jnp.float32
            )
            result.append(both[:size] + both[size:])
        return result

    def direct(it, dz, *flips):
        sums = [None] * cols
        for d in flips:
            b = across(dz) * planes + flipped(d)
            right = spread(gath[it, dz, d]).astype(jnp.bfloat16)
            for dc in range(cols):
                high, low = split_tile((col + dc) % cols * rows + b)
                term = jnp.dot(high, right, preferred_element_type=jnp.float32) + jnp.dot(
                    low, right, preferred_element_type=jnp.float32
                )
                sums[dc] = term if sums[dc] is None else sums[dc] + term
        for dc in range(cols):
            total[dc] += sums[dc]

    def begin(it):
        lhs[0] = spread(gath[it, 0, 0]).T.astype(jnp.bfloat16)
        total[...] = jnp.zeros_like(total)
        direct(it, 0, 0)

    def blocked(it, dz, d, fresh=False):
        right = spread(gath[it, dz, d]).astype(jnp.bfloat16)
        for dc, part in enumerate(terms(dz, d, right, *range(cols))):
            if fresh:
                total[dc] = part
            else:
                total[dc] += part

    if planned:
        parts[count] = jnp.zeros((2 * size, size), jnp.bfloat16)
        for i, load in enumerate(loads):
            load.wait()

            def cut(slot, carry):
                block = tiles[slot]
                high = block.astype(jnp.bfloat16)
                parts[slot, pl.ds(0, size)] = high
                parts[slot, pl.ds(size, size)] = (block - high.astype(jnp.float32)).astype(
                    jnp.bfloat16
                )
                return carry

            lax.fori_loop(i * share, (i + 1) * share, cut, 0)
        fill.wait()
        blocked(0, 0, 0, True)
    else:
        for load in loads:
            load.wait()
        fill.wait()
        begin(0)
    pl.semaphore_wait(barrier, (lines - 1) + 2 + (cols - 1))

    def finish_sends(it):
        for dz in range(lines):
            for h in range(2):
                if dz > 0:
                    ag_line_half(it, dz, h).wait_send()
                    rs_line_half(it, dz, h).wait_send()
                for d in range(1, 3):
                    ag_plane_half(it, dz, d, h).wait_send()
                    rs_plane(it, dz, d, h).wait_send()
                if dz not in AG_DIAG:
                    ag_turn(it, dz, h).wait_send()
                if dz not in RS_DIAG:
                    rs_turn(it, dz, h).wait_send()
            if dz in AG_DIAG:
                ag_diag(it, dz).wait_send()
            if dz in RS_DIAG:
                rs_diag(it, dz).wait_send()

    def ordered(it):
        arrived = set()
        opening = next(task for task in ORDER if task[0] == "D")

        def once(copy, *key):
            if key not in arrived:
                arrived.add(key)
                copy(it, *key[1:]).wait_recv()

        def gathered(dz, d, q):
            if PAIR and dz == 1:
                once(lambda it, dz, d, q: ag_pair_half(it, d, q), "ap", dz, d, q)
            else:
                once(ag_plane_half, "ap", dz, d, q)

        def reduced(dz, d, q):
            once(rs_plane, "rp", dz, d, q)

        if it == 0:
            for dc in range(1, cols):
                col_x(it, dc).start()
        for place, task in enumerate(ORDER):
            kind, args = task[0], task[1:]
            if it > 0 and place == len(ORDER) // 2:
                finish_sends(it - 1)
            if kind == "AL":
                ag_line_half(it, *args).start()
            elif kind == "AP":
                ag_plane_half(it, 0, *args).start()
            elif kind == "LHS":
                own = spread(gath[it, 0, 0]).T.astype(jnp.bfloat16)
                if it == 0:
                    col_x(it, 1).wait_recv()
                    near = rowg[it, 1]
                else:
                    col_s(it - 1).wait_recv()
                    near = rrecv[it - 1, 0] + rpart[it - 1, 1]
                near = spread(near).T.astype(jnp.bfloat16)
                first = jnp.where(col == 0, own, near)
                second = jnp.where(col == 0, near, own)
                stack[...] = jnp.concatenate([first, first, second, second], axis=1)
            elif kind == "C":
                dz, = args
                zsend[it, dz, 3] = mirrored(it, dz, 3)
                if dz in RS_DIAG:
                    rs_diag(it, dz).start()
                else:
                    for h in range(2):
                        rs_turn(it, dz, h).start()
            elif kind == "E":
                dz, d = args
                zsend[it, dz, d] = mirrored(it, dz, d)
                for q in range(2 if dz in RS_DIAG else 1):
                    if PAIR and dz == 1:
                        rs_pair(it, d, q).start()
                    elif dz > 0 or not PAIR:
                        rs_plane(it, dz, d, q).start()
            elif kind == "L":
                dz, d = args
                once(rs_turn, "rt", dz, d % 2)
                zsend[it, dz, d, piece(d)] += zrecv[it, dz, 3, piece(d)]
                if PAIR and dz == 1:
                    rs_pair(it, d, 1).start()
                else:
                    rs_plane(it, dz, d, 1).start()
            elif kind == "S":
                d, q = args
                part = piece(d - 1 + q)
                once(lambda it, dz, d, q: rs_pair(it, d, q), "rp", 1, d, q)
                more = zrecv[it, 1, d, part]
                if q == 1 and 0 not in RS_DIAG:
                    once(rs_turn, "rt", 0, d % 2)
                    more = more + zrecv[it, 0, 3, part]
                zsend[it, 0, d, part] += more
                rs_plane(it, 0, d, q).start()
            elif kind == "M":
                dz, = args
                z2send[it, dz] = mirrored(it, dz, 0)
            elif kind == "RL":
                dz, p = args
                part = piece(p)
                if dz > 1 or not PAIR:
                    reduced(dz, 1, p)
                    reduced(dz, 2, 1 - p)
                    z2send[it, dz, part] += zrecv[it, dz, 1, part] + zrecv[it, dz, 2, part]
                if dz in RS_DIAG:
                    once(rs_diag, "rd", dz)
                    z2send[it, dz, part] += zrecv[it, dz, 3, part]
                rs_line_half(it, dz, p).start()
            elif kind == "G":
                for d in range(1, 3):
                    for q in range(2):
                        reduced(0, d, q)
                z2send[it, 0] += zrecv[it, 0, 1] + zrecv[it, 0, 2]
                if 0 in RS_DIAG:
                    once(rs_diag, "rd", 0)
                    z2send[it, 0] += zrecv[it, 0, 3]
            elif kind == "FR":
                wide = z2send[it, 0]
                for dz in range(1, lines):
                    for p in range(2):
                        once(rs_line_half, "rl", dz, p)
                    wide = wide + z2recv[it, dz]
                z2send[it, 0] = pack_tall(unpack_wide(wide, vecs, size))
            elif kind == "AF":
                dz, d, q = args
                if PAIR and dz == 1:
                    gathered(0, d, q)
                    ag_pair_half(it, d, q).start()
                else:
                    once(ag_line_half, "al", dz, (d - 1 + q) % 2)
                    ag_plane_half(it, dz, d, q).start()
            elif kind == "AT":
                dz, h = args
                gathered(dz, 1 + h, 0)
                ag_turn(it, dz, h).start()
            elif kind == "AD":
                dz, = args
                if dz > 0:
                    for p in range(2):
                        once(ag_line_half, "al", dz, p)
                ag_diag(it, dz).start()
            elif it > 0 or args != (0, 0):
                dz, d = args
                if d == 0 and dz > 0:
                    for p in range(2):
                        once(ag_line_half, "al", dz, p)
                elif d in (1, 2):
                    for q in range(2):
                        gathered(dz, d, q)
                elif d == 3 and dz in AG_DIAG:
                    once(ag_diag, "ad", dz)
                elif d == 3:
                    for h in range(2):
                        once(ag_turn, "at", dz, h)
                if place < len(ORDER) - 1:
                    blocked(it, dz, d, it > 0 and task == opening)
        right = spread(gath[it, dz, d]).astype(jnp.bfloat16)
        rpart[it, 1] = fold_tall(total[1] + terms(dz, d, right, 1)[0])
        col_y(it, 1).start()
        mine = fold_tall(total[0] + terms(dz, d, right, 0)[0]) + z2send[it, 0]
        if it < ITERS - 1:
            rpart[it, 0] = mine
            col_s(it).start()
        if it == ITERS - 1:
            finish_sends(it)
        col_y(it, 1).wait_recv()
        return mine + rrecv[it, 1]

    def product(it):
        for dz in range(1, lines):
            ag_line(it, dz).start()
        fresh = it == 0 or not paired
        if fresh:
            for dc in range(1, cols):
                col_x(it, dc).start()
        for d in range(1, 3):
            ag_plane(it, 0, d).start()
        if it > 0:
            begin(it)
        if fresh:
            for dc in range(1, cols):
                col_x(it, dc).wait_recv()
                lhs[dc] = spread(rowg[it, dc]).T.astype(jnp.bfloat16)
        else:
            col_s(it - 1).wait_recv()
            near = rrecv[it - 1, 0] + rpart[it - 1, 1]
            lhs[1] = spread(near).T.astype(jnp.bfloat16)

        def corner(n, carry):
            dz = lines - 1 - n
            zsend[it, dz, 3] = mirrored(it, dz, 3)
            for h in range(2):
                rs_turn(it, dz, h).start()
            return carry

        lax.fori_loop(0, lines, corner, 0)

        def early(n, carry):
            dz = (lines - n) % lines
            for d in range(1, 3):
                zsend[it, dz, d] = mirrored(it, dz, d)
                rs_plane(it, dz, d, 0).start()
            return carry

        def late(dz):
            for d in range(1, 3):
                part = pl.ds(d % 2 * quarter, quarter)
                rs_turn(it, dz, d % 2).wait_recv()
                zsend[it, dz, d, part] += zrecv[it, dz, 3, part]
                rs_plane(it, dz, d, 1).start()

        def forward(dz, carry):
            back = lines - dz
            late(back)
            ag_line(it, dz).wait_recv()
            for d in range(1, 3):
                ag_plane(it, dz, d).start()
            z2send[it, back] = mirrored(it, back, 0)
            direct(it, dz, 0)
            return carry

        def turn(dz):
            for h in range(2):
                ag_plane(it, dz, 1 + h).wait_recv()
                ag_turn(it, dz, h).start()

        def gather_plane(dz):
            for d in range(1, 3):
                for k in range(2):
                    rs_plane(it, dz, d, k).wait_recv()
            z2send[it, dz] += zrecv[it, dz, 1] + zrecv[it, dz, 2]

        def settle(dz, carry):
            gather_plane(lines - dz)
            rs_line(it, lines - dz).start()
            turn(dz)
            direct(it, dz, 1, 2)
            return carry

        lax.fori_loop(1, lines, early, 0)
        lax.fori_loop(1, lines, forward, 0)
        early(0, 0)
        late(0)
        z2send[it, 0] = mirrored(it, 0, 0)
        turn(0)
        direct(it, 0, 1, 2)
        lax.fori_loop(1, lines, settle, 0)
        gather_plane(0)

        def last(dz, carry):
            for h in range(2):
                ag_turn(it, dz, h).wait_recv()
            direct(it, dz, 3)
            return carry

        lax.fori_loop(0, lines, last, 0)

        for dc in range(1, cols):
            rpart[it, dc] = fold_tall(total[dc])
            col_y(it, dc).start()
        mine = fold_tall(total[0])
        wide = z2send[it, 0]
        for dz in range(1, lines):
            rs_line(it, dz).wait_recv()
            wide = wide + z2recv[it, dz]
        mine = mine + pack_tall(unpack_wide(wide, vecs, size))
        if paired and it < ITERS - 1:
            rpart[it, 0] = mine
            col_s(it).start()
        for dc in range(1, cols):
            col_y(it, dc).wait_recv()
            mine = mine + rrecv[it, dc]
        return mine

    for it in range(ITERS):
        result = ordered(it) if planned else product(it)
        if it < ITERS - 1:
            gath[it + 1, 0, 0] = result
        else:
            tall = jnp.concatenate([result[:, :vecs], result[:, vecs:]], axis=0)
            out_ref[:, pl.ds(0, LANES)] = tall[:LANES].T
            out_ref[:, pl.ds(LANES, size - LANES)] = tall[LANES:].T

    for it in range(ITERS):
        for dc in range(1, cols):
            if it == 0 or not paired:
                col_x(it, dc).wait_send()
            col_y(it, dc).wait_send()
        if paired and it < ITERS - 1:
            col_s(it).wait_send()

    def drain(it, carry):
        for dz in range(1, lines):
            ag_line(it, dz).wait_send()
            rs_line(it, dz).wait_send()

        def plane_sends(dz, inner):
            for d in range(1, 3):
                ag_plane(it, dz, d).wait_send()
                for k in range(2):
                    rs_plane(it, dz, d, k).wait_send()
            for h in range(2):
                ag_turn(it, dz, h).wait_send()
                rs_turn(it, dz, h).wait_send()
            return inner

        return lax.fori_loop(0, lines, plane_sends, carry)

    if not planned:
        lax.fori_loop(0, ITERS, drain, 0)


def local(rows, cols, vectors, stiff_tiles, tile_coords, tile_valid):
    size, vecs = vectors.shape
    count = stiff_tiles.shape[2]
    planes = 4
    lines = rows // planes
    kept = lines == 4 and cols == 2 and count % CHUNKS == 0 and count <= 64
    block = (size * vecs // LANES, LANES)
    f32 = jnp.float32
    dma = pltpu.SemaphoreType.DMA
    grid = (ITERS, lines, planes)
    return pl.pallas_call(
        functools.partial(kernel, rows, cols, planes, kept),
        out_shape=pltpu.VMEM((vecs, size), f32),
        in_specs=[
            pl.BlockSpec(memory_space=pl.ANY),
            pl.BlockSpec(memory_space=pl.ANY),
            pl.BlockSpec(memory_space=pl.ANY),
            pl.BlockSpec(memory_space=pl.ANY),
        ],
        out_specs=pl.BlockSpec(memory_space=pltpu.VMEM),
        scratch_shapes=[
            pltpu.VMEM((vecs, size), f32),
            pltpu.VMEM((2, count), jnp.int32),
            pltpu.VMEM((1, count), jnp.int32),
            pltpu.VMEM((rows * cols, LANES), jnp.int32),
            pltpu.SMEM((rows * cols, LANES), jnp.int32),
            pltpu.VMEM((count, size, size), f32),
            pltpu.VMEM(grid + block, f32),
            pltpu.VMEM((ITERS, cols) + block, f32),
            pltpu.VMEM((ITERS, cols) + block, f32),
            pltpu.VMEM((ITERS, cols) + block, f32),
            pltpu.VMEM(grid + block, f32),
            pltpu.VMEM(grid + block, f32),
            pltpu.VMEM((ITERS, lines) + block, f32),
            pltpu.VMEM((ITERS, lines) + block, f32),
            pltpu.VMEM((cols, 2 * vecs, size), jnp.bfloat16),
            pltpu.VMEM((cols, size, 2 * vecs), f32),
            pltpu.VMEM((count + 1 if kept else 1, 2 * size, size), jnp.bfloat16),
            pltpu.VMEM((2 * vecs, 4 * size), jnp.bfloat16),
            dma((CHUNKS,)),
            dma((4,)),
            dma(grid + (2,)), dma(grid + (2,)),
            dma((ITERS, lines, 2)), dma((ITERS, lines, 2)),
            dma((ITERS, cols)), dma((ITERS, cols)),
            dma(grid + (2,)), dma(grid + (2,)),
            dma((ITERS, lines, 2)), dma((ITERS, lines, 2)),
            dma((ITERS, lines, 2)), dma((ITERS, lines, 2)),
            dma((ITERS, cols)), dma((ITERS, cols)),
        ],
        compiler_params=pltpu.CompilerParams(
            collective_id=0, has_side_effects=True, vmem_limit_bytes=60 * 1024 * 1024
        ),
    )(vectors.T, tile_coords[0, 0].T, tile_valid[0], stiff_tiles[0, 0]).T


def solution(mesh):
    placed = (
        P(("row", "col"), None),
        P("row", "col", None, None, None),
        P("row", "col", None, None),
        P("row", "col", None),
    )
    return jax.shard_map(
        functools.partial(local, mesh.shape["row"], mesh.shape["col"]),
        mesh=mesh, in_specs=placed, out_specs=P(("row", "col"), None), check_vma=False,
    )
```
